32 devices in a mesh: node: 4 (over y, x), space: 8 (over z, core).
Axes of the slice: x: 2, y: 2, z: 4, core: 2. Of those that a mesh axis runs over, the one named last changes fastest.
Arguments:
- snapshots: bfloat16 [512, 16, 8192], P('node', 'space'), may hold values from -8 to 8
- kappa: bfloat16 [16, 8192], P('space'), may hold values from 0.099609375 to 10
Outputs:
- gram: float32 [512, 512], P('node', 'space')
The draws below stay inside these ranges and needn't reach their ends.
All inputs are finite; a program needn't handle non-finite values.
Results may differ from the reference program's by a relative error of at most 0.0003.
Values may be sent and summed in bfloat16 or wider, within the bound.
A program may use at most 128 MiB of HBM per device.

```python
import math
import jax
import jax.numpy as jnp
from jax import lax

SNAP_DEV = 128
NY = 128
NZ = 64
SNAPS = 512
NX = 16


def draw_snapshots(key, part):
    key_common = jax.random.fold_in(key, 11)
    key_noise = jax.random.fold_in(key, 12)
    key_weight = jax.random.fold_in(key, 13)
    key_planes = jax.random.fold_in(key, 14)
    plane_gain = jax.random.uniform(key_planes, (NX, 1), jnp.float32, 0.4, 1.6)
    common = jnp.clip(jax.random.normal(key_common, (1, NY * NZ), jnp.float32), -2.5, 2.5)
    noise = jnp.clip(jax.random.normal(key_noise, (SNAPS, NX, NY * NZ), jnp.float32), -4.0, 4.0)
    weights = jax.random.uniform(key_weight, (SNAPS, 1, 1), jnp.float32, -1.0, 1.0)
    field = plane_gain * common
    return (weights * field[None] + noise).astype(jnp.bfloat16)


def level_of(key, dims, cuts, low, high):
    factor_of = 1.0
    for position, blocks in cuts:
        steps = jax.random.uniform(jax.random.fold_in(jax.random.fold_in(key, 6), position), (blocks,), jnp.float32, low / len(cuts), high / len(cuts))
        factor_of = factor_of * jnp.repeat(jnp.exp(steps), dims[position] // blocks).reshape((-1,) + (1,) * (len(dims) - 1 - position))
    return factor_of


def setup_inputs(seed: int = 0) -> dict:
    splits = jax.random.split(jax.random.key(seed), 3)
    snapshots = draw_snapshots(jax.random.fold_in(splits[2], 71), 0)
    kappa = jnp.clip(jnp.exp(math.log(10.0) - 4.609084 * jax.random.uniform(splits[1], (NX, NY * NZ), jnp.float32) ** level_of(splits[1], (NX, NY * NZ), ((0, 8),), -0.2, 0.2)), 0.099609375, 10.0).astype(jnp.bfloat16)
    return dict(snapshots=snapshots, kappa=kappa)


def ahead(values, offset):
    tail = jnp.zeros(values.shape[:-1] + (offset,), values.dtype)
    return jnp.concatenate([values[..., offset:], tail], axis=-1)

def behind(values, offset):
    head = jnp.zeros(values.shape[:-1] + (offset,), values.dtype)
    return jnp.concatenate([head, values[..., :-offset]], axis=-1)

def flat_terms(field, kap_mid):
    width = field.shape[-1]
    zpos = jnp.arange(width, dtype=jnp.int32) % NZ
    up_ok = zpos != NZ - 1
    down_ok = zpos != 0
    total = jnp.zeros(field.shape, jnp.float32)
    near = jnp.where(up_ok, ahead(field, 1), 0.0)
    near_k = jnp.where(up_ok, ahead(kap_mid, 1), 0.0)
    total = total + 0.5 * (kap_mid + near_k) * (field - near)
    near = jnp.where(down_ok, behind(field, 1), 0.0)
    near_k = jnp.where(down_ok, behind(kap_mid, 1), 0.0)
    total = total + 0.5 * (kap_mid + near_k) * (field - near)
    total = total + 0.5 * (kap_mid + ahead(kap_mid, NZ)) * (field - ahead(field, NZ))
    total = total + 0.5 * (kap_mid + behind(kap_mid, NZ)) * (field - behind(field, NZ))
    return total

def stiffness(block, kap):
    padded = jnp.pad(block, ((0, 0), (1, 1), (0, 0)))
    kpad = jnp.pad(kap, ((1, 1), (0, 0)))
    total = flat_terms(block, kap)
    total = total + 0.5 * (kap + kpad[:-2]) * (block - padded[:, :-2])
    total = total + 0.5 * (kap + kpad[2:]) * (block - padded[:, 2:])
    return total

def reference(snapshots, kappa):
    kap = kappa.astype(jnp.float32)
    blocks = snapshots.reshape(SNAPS // SNAP_DEV, SNAP_DEV, NX, NY * NZ)
    image = lax.map(lambda b: stiffness(b.astype(jnp.float32), kap).astype(jnp.bfloat16), blocks)
    image = image.reshape(SNAPS, NX * NY * NZ)
    flat = snapshots.reshape(SNAPS, NX * NY * NZ)
    gram = jnp.dot(image, flat.T, preferred_element_type=jnp.float32)
    return gram * jnp.float32(1.0 / math.sqrt(NX * NY * NZ))
```

```python
import functools
import math

import jax
import jax.numpy as jnp
from jax import lax
from jax.experimental import pallas as pl
from jax.experimental.pallas import tpu as pltpu
from jax.sharding import PartitionSpec as P

NY = 128
NZ = 64
LANE = 128
ROWS = 16
MESH = pl.DeviceIdType.MESH


def packed(values, nodes):
    length = values.shape[-1] // nodes
    main = values.reshape(values.shape[:-1] + (nodes, length))
    none = jnp.zeros(main.shape[:-2] + (1, NZ), values.dtype)
    before = jnp.concatenate([none, main[..., :-1, -NZ:]], axis=-2)
    after = jnp.concatenate([main[..., 1:, :NZ], none], axis=-2)
    return jnp.concatenate([main, before, after], axis=-1)


def gram_kernel(
    nodes, spaces, xs_ref, kap_ref, out_ref,
    held, side, kside, coef, image,
    own_sem, send_sem, recv_sem, hsend, hrecv, ksend, krecv,
):
    me = lax.axis_index("node")
    at = lax.axis_index("space")
    snap_rows = xs_ref.shape[1]
    full = xs_ref.shape[2] // 2
    length = full - LANE
    tiles = length // LANE
    chunks = snap_rows // ROWS
    has_low = at > 0
    has_high = at < spaces - 1

    barrier = pltpu.get_barrier_semaphore()
    for turn in range(1, nodes):
        pl.semaphore_signal(
            barrier, inc=1, device_id={"node": lax.rem(me + turn, nodes)}, device_id_type=MESH
        )

    @pl.when(has_low)
    def _():
        pl.semaphore_signal(barrier, inc=1, device_id={"space": at - 1}, device_id_type=MESH)

    @pl.when(has_high)
    def _():
        pl.semaphore_signal(barrier, inc=1, device_id={"space": at + 1}, device_id_type=MESH)

    @pl.when(jnp.logical_not(has_low))
    def _():
        side[0] = jnp.zeros(side.shape[1:], side.dtype)
        kside[0] = jnp.zeros(kside.shape[1:], kside.dtype)

    @pl.when(jnp.logical_not(has_high))
    def _():
        side[1] = jnp.zeros(side.shape[1:], side.dtype)
        kside[1] = jnp.zeros(kside.shape[1:], kside.dtype)

    both = jnp.logical_and(has_low, has_high)

    @pl.when(both)
    def _():
        pl.semaphore_wait(barrier, nodes + 1)

    @pl.when(jnp.logical_not(both))
    def _():
        pl.semaphore_wait(barrier, nodes)

    def own_copy(chunk):
        rows = pl.ds(chunk * ROWS, ROWS)
        return pltpu.make_async_copy(
            xs_ref.at[me, rows], held.at[me, rows], own_sem.at[chunk]
        )

    def block_copy(chunk, turn):
        rows = pl.ds(chunk * ROWS, ROWS)
        peer = lax.rem(me + turn, nodes)
        return pltpu.make_async_remote_copy(
            src_ref=xs_ref.at[peer, rows],
            dst_ref=held.at[me, rows],
            send_sem=send_sem.at[turn - 1, chunk],
            recv_sem=recv_sem.at[turn - 1, chunk],
            device_id={"node": peer},
            device_id_type=MESH,
        )

    def side_copy(chunk, high):
        rows = pl.ds(chunk * ROWS, ROWS)
        return pltpu.make_async_remote_copy(
            src_ref=held.at[:, rows, pl.ds(full if high else 0, length)],
            dst_ref=side.at[0 if high else 1, :, rows],
            send_sem=hsend.at[0 if high else 1, chunk],
            recv_sem=hrecv.at[0 if high else 1, chunk],
            device_id={"space": at + 1 if high else at - 1},
            device_id_type=MESH,
        )

    def kappa_copy(high):
        return pltpu.make_async_remote_copy(
            src_ref=kap_ref.at[1 if high else 0],
            dst_ref=kside.at[0 if high else 1],
            send_sem=ksend.at[0 if high else 1],
            recv_sem=krecv.at[0 if high else 1],
            device_id={"space": at + 1 if high else at - 1},
            device_id_type=MESH,
        )

    @pl.when(has_high)
    def _():
        kappa_copy(True).start()

    @pl.when(has_low)
    def _():
        kappa_copy(False).start()

    def begin(chunk, carry):
        own_copy(chunk).start()
        for turn in range(1, nodes):
            block_copy(chunk, turn).start()
        return carry

    lax.fori_loop(0, chunks, begin, 0)

    @pl.when(has_high)
    def _():
        kappa_copy(True).wait_send()
        kappa_copy(False).wait_recv()

    @pl.when(has_low)
    def _():
        kappa_copy(False).wait_send()
        kappa_copy(True).wait_recv()

    lane = lax.broadcasted_iota(jnp.int32, (8, LANE), 1)
    lower = lane < NZ
    zpos = lane % NZ
    inner = jnp.where(zpos == NZ - 1, 0.0, 0.5).astype(jnp.float32)
    edge = jnp.where(zpos == 0, 0.5, jnp.where(zpos == NZ - 1, 0.5, 0.0)).astype(jnp.float32)

    def cols(tile, plane=0):
        return pl.ds(plane * full + tile * LANE, LANE)

    for plane in range(2):
        kap = [kap_ref[plane, :, cols(t)] for t in range(tiles + 1)]
        turned = [pltpu.roll(k, NZ, 1) for k in kap[:tiles]]
        for t in range(tiles):
            k = kap[t]
            up = jnp.where(lower, turned[t], turned[t + 1] if t + 1 < tiles else kap[tiles])
            down = jnp.where(lower, turned[t - 1] if t else kap[tiles], turned[t])
            coef[4 * plane, :, cols(t)] = inner * (k + pltpu.roll(k, LANE - 1, 1))
            coef[4 * plane + 1, :, cols(t)] = 0.5 * (k + up)
            coef[4 * plane + 2, :, cols(t)] = 0.5 * (k + down)
            coef[4 * plane + 3, :, cols(t)] = edge * k
    for t in range(tiles):
        low, high = (kap_ref[0, :, cols(t)], kap_ref[1, :, cols(t)])
        coef[8, :, cols(t)] = 0.5 * (low + kside[0, :, cols(t)])
        coef[9, :, cols(t)] = 0.5 * (low + high)
        coef[10, :, cols(t)] = 0.5 * (high + kside[1, :, cols(t)])

    def arrive(chunk):
        own_copy(chunk).wait()
        for turn in range(1, nodes):
            block_copy(chunk, turn).wait_recv()

        @pl.when(has_high)
        def _():
            side_copy(chunk, True).start()

        @pl.when(has_low)
        def _():
            side_copy(chunk, False).start()

    lower3 = lax.broadcasted_iota(jnp.int32, (ROWS // 8, 8, LANE), 2) < NZ

    def apply(chunk):
        @pl.when(has_high)
        def _():
            side_copy(chunk, False).wait_recv()

        @pl.when(has_low)
        def _():
            side_copy(chunk, True).wait_recv()

        rows = pl.ds(chunk * ROWS, ROWS)

        def one(node, carry):
            def wide(value):
                return value.astype(jnp.float32).reshape(ROWS // 8, 8, LANE)

            def load(plane, tile):
                return wide(held[node, rows, cols(tile, plane)])

            sides = [load(plane, tiles) for plane in range(2)]
            now = [load(plane, 0) for plane in range(2)]
            turned = [pltpu.roll(v, NZ, 2) for v in now]
            last = list(sides)
            for t in range(tiles):
                if t + 1 < tiles:
                    later = [load(plane, t + 1) for plane in range(2)]
                    coming = [pltpu.roll(v, NZ, 2) for v in later]
                else:
                    later, coming = (None, list(sides))
                mid = coef[9, :, cols(t)] * (now[0] - now[1])
                beside = [wide(side[p, node, rows, cols(t)]) for p in range(2)]
                for plane in range(2):
                    v = now[plane]
                    up = jnp.where(lower3, turned[plane], coming[plane])
                    down = jnp.where(lower3, last[plane], turned[plane])
                    flux = coef[4 * plane, :, cols(t)] * (v - pltpu.roll(v, LANE - 1, 2))
                    total = flux - pltpu.roll(flux, 1, 2)
                    total = total + coef[4 * plane + 3, :, cols(t)] * v
                    total = total + coef[4 * plane + 1, :, cols(t)] * (v - up)
                    total = total + coef[4 * plane + 2, :, cols(t)] * (v - down)
                    total = total + coef[8 + 2 * plane, :, cols(t)] * (v - beside[plane])
                    total = total - mid if plane else total + mid
                    image[node, rows, cols(t, plane)] = total.reshape(ROWS, LANE).astype(
                        jnp.bfloat16
                    )
                last, turned, now = (turned, coming, later)
            for plane in range(2):
                image[node, rows, cols(tiles, plane)] = jnp.zeros((ROWS, LANE), jnp.bfloat16)
            return carry

        lax.fori_loop(0, nodes, one, 0)

    arrive(0)

    def step(chunk, carry):
        arrive(chunk)
        apply(chunk - 1)
        return carry

    lax.fori_loop(1, chunks, step, 0)
    apply(chunks - 1)

    def product(index, carry):
        block, half = (index // 2, index % 2)
        left = image[pl.ds(block, 1)].reshape(snap_rows, 2 * full)
        right = held[pl.ds(half * 2, 2)].reshape(2 * snap_rows, 2 * full)
        tile = lax.dot_general(
            left, right, (((1,), (1,)), ((), ())), preferred_element_type=jnp.float32
        )
        out_ref[
            pl.ds(pl.multiple_of(block * snap_rows, snap_rows), snap_rows),
            pl.ds(pl.multiple_of(half * 2 * snap_rows, 2 * snap_rows), 2 * snap_rows),
        ] = tile
        return carry

    lax.fori_loop(0, 2 * nodes, product, 0)

    def finish(chunk, carry):
        for turn in range(1, nodes):
            block_copy(chunk, turn).wait_send()

        @pl.when(has_high)
        def _():
            side_copy(chunk, True).wait_send()

        @pl.when(has_low)
        def _():
            side_copy(chunk, False).wait_send()

        return carry

    lax.fori_loop(0, chunks, finish, 0)


def per_device(snapshots, kappa):


    snap_rows, planes, width = snapshots.shape
    nodes, spaces = (lax.axis_size("node"), lax.axis_size("space"))
    length = width // nodes
    full = length + LANE
    chunks = snap_rows // ROWS
    xs = packed(snapshots, nodes)
    xs = jnp.transpose(xs, (2, 0, 1, 3)).reshape(nodes, snap_rows, planes * full)
    kap = packed(kappa.astype(jnp.float32), nodes)
    kap = lax.dynamic_index_in_dim(kap, lax.axis_index("node"), axis=1, keepdims=True)
    kap = jnp.broadcast_to(kap, (planes, 8, full))
    order = nodes * snap_rows
    partial_rows = pl.pallas_call(
        functools.partial(gram_kernel, nodes, spaces),
        out_shape=jax.ShapeDtypeStruct((order, order), jnp.float32),
        in_specs=[
            pl.BlockSpec(memory_space=pl.ANY),
            pl.BlockSpec(memory_space=pltpu.VMEM),
        ],
        out_specs=pl.BlockSpec(memory_space=pltpu.VMEM),
        scratch_shapes=[
            pltpu.VMEM((nodes, snap_rows, planes * full), jnp.bfloat16),
            pltpu.VMEM((2, nodes, snap_rows, length), jnp.bfloat16),
            pltpu.VMEM((2, 8, full), jnp.float32),
            pltpu.VMEM((11, 8, length), jnp.float32),
            pltpu.VMEM((nodes, snap_rows, planes * full), jnp.bfloat16),
            pltpu.SemaphoreType.DMA((chunks,)),
            pltpu.SemaphoreType.DMA((nodes - 1, chunks)),
            pltpu.SemaphoreType.DMA((nodes - 1, chunks)),
            pltpu.SemaphoreType.DMA((2, chunks)),
            pltpu.SemaphoreType.DMA((2, chunks)),
            pltpu.SemaphoreType.DMA((2,)),
            pltpu.SemaphoreType.DMA((2,)),
        ],
        compiler_params=pltpu.CompilerParams(
            collective_id=0, has_side_effects=True, vmem_limit_bytes=40 * 1024 * 1024
        ),
        name="gram_parts",
    )(xs, kap)
    mine = lax.psum_scatter(partial_rows, "node", scatter_dimension=0, tiled=True)
    gram = lax.psum_scatter(mine, "space", scatter_dimension=1, tiled=True)
    return gram * jnp.float32(1.0 / math.sqrt(planes * spaces * NY * NZ))


def solution(mesh):
    placed = (P("node", "space", None), P("space", None))
    return jax.shard_map(
        per_device, mesh=mesh, in_specs=placed, out_specs=P("node", "space"), check_vma=False
    )
```

```python
import functools
import math

import jax
import jax.numpy as jnp
from jax import lax
from jax.experimental import pallas as pl
from jax.experimental.pallas import tpu as pltpu
from jax.sharding import PartitionSpec as P

NY = 128
NZ = 64
LANE = 128
ROWS = 16
MESH = pl.DeviceIdType.MESH


def gram_kernel(
    nodes, spaces, scale, snap_ref, kap_ref, out_ref,
    held, ends, ends_out, edge, side, kside, coef, image, gram, first, second, third, fourth,
    own_sem, edge_sem, send_sem, recv_sem, esend, erecv, hsend, hrecv, ksend, krecv,
    send1, recv1, send2, recv2, send3, recv3, send4, recv4,
):
    me = lax.axis_index("node")
    at = lax.axis_index("space")
    snap_rows = snap_ref.shape[1]
    length = snap_ref.shape[2] // nodes
    tiles = length // LANE
    chunks = snap_rows // ROWS
    has_low = at > 0
    has_high = at < spaces - 1
    summed = out_ref.shape[0] == snap_rows
    layers = spaces // 2 if summed else 1

    def edge_copy(index):
        return pltpu.make_async_copy(
            snap_ref.at[:, :, pl.ds((index + 1) * length - LANE, 2 * LANE)],
            edge.at[index],
            edge_sem.at[index],
        )

    for index in range(nodes - 1):
        edge_copy(index).start()

    barrier = pltpu.get_barrier_semaphore()
    for turn in range(1, nodes):
        pl.semaphore_signal(
            barrier, inc=1, device_id={"node": lax.rem(me + turn, nodes)}, device_id_type=MESH
        )
    for turn in range(1, layers):
        pl.semaphore_signal(
            barrier,
            inc=1,
            device_id={"space": lax.rem(at + 2 * turn, spaces)},
            device_id_type=MESH,
        )

    @pl.when(has_low)
    def _():
        pl.semaphore_signal(barrier, inc=1, device_id={"space": at - 1}, device_id_type=MESH)

    @pl.when(has_high)
    def _():
        pl.semaphore_signal(barrier, inc=1, device_id={"space": at + 1}, device_id_type=MESH)

    @pl.when(jnp.logical_not(has_low))
    def _():
        side[0] = jnp.zeros(side.shape[1:], side.dtype)
        kside[0] = jnp.zeros(kside.shape[1:], kside.dtype)

    @pl.when(jnp.logical_not(has_high))
    def _():
        side[1] = jnp.zeros(side.shape[1:], side.dtype)
        kside[1] = jnp.zeros(kside.shape[1:], kside.dtype)

    both = jnp.logical_and(has_low, has_high)

    @pl.when(both)
    def _():
        pl.semaphore_wait(barrier, nodes + layers)

    @pl.when(jnp.logical_not(both))
    def _():
        pl.semaphore_wait(barrier, nodes + layers - 1)

    def own_copy(chunk):
        rows = pl.ds(chunk * ROWS, ROWS)
        return pltpu.make_async_copy(
            snap_ref.at[:, rows, pl.ds(pl.multiple_of(me * length, LANE), length)],
            held.at[me, :, rows],
            own_sem.at[chunk],
        )

    def block_copy(chunk, turn):
        rows = pl.ds(chunk * ROWS, ROWS)
        peer = lax.rem(me + turn, nodes)
        return pltpu.make_async_remote_copy(
            src_ref=snap_ref.at[:, rows, pl.ds(pl.multiple_of(peer * length, LANE), length)],
            dst_ref=held.at[me, :, rows],
            send_sem=send_sem.at[turn - 1, chunk],
            recv_sem=recv_sem.at[turn - 1, chunk],
            device_id={"node": peer},
            device_id_type=MESH,
        )

    def side_copy(chunk, high):
        rows = pl.ds(chunk * ROWS, ROWS)
        return pltpu.make_async_remote_copy(
            src_ref=held.at[:, 1 if high else 0, rows],
            dst_ref=side.at[0 if high else 1, :, rows],
            send_sem=hsend.at[0 if high else 1, chunk],
            recv_sem=hrecv.at[0 if high else 1, chunk],
            device_id={"space": at + 1 if high else at - 1},
            device_id_type=MESH,
        )

    def kappa_copy(high):
        return pltpu.make_async_remote_copy(
            src_ref=kap_ref.at[1 if high else 0, :, pl.ds(pl.multiple_of(me * length, LANE), length)],
            dst_ref=kside.at[0 if high else 1],
            send_sem=ksend.at[0 if high else 1],
            recv_sem=krecv.at[0 if high else 1],
            device_id={"space": at + 1 if high else at - 1},
            device_id_type=MESH,
        )

    def ends_copy(turn):
        peer = lax.rem(me + turn, nodes)
        return pltpu.make_async_remote_copy(
            src_ref=ends_out.at[peer],
            dst_ref=ends.at[me],
            send_sem=esend.at[turn - 1],
            recv_sem=erecv.at[turn - 1],
            device_id={"node": peer},
            device_id_type=MESH,
        )

    @pl.when(has_high)
    def _():
        kappa_copy(True).start()

    @pl.when(has_low)
    def _():
        kappa_copy(False).start()

    def begin(chunk, carry):
        own_copy(chunk).start()
        for turn in range(1, nodes):
            block_copy(chunk, turn).start()
        return carry

    begin(0, 0)
    for index in range(nodes - 1):
        edge_copy(index).wait()

    wide_lower = lax.broadcasted_iota(jnp.int32, (snap_rows, LANE), 1) < NZ
    for dest in range(nodes):
        for plane in range(2):
            before = after = jnp.zeros((snap_rows, LANE), jnp.float32)
            if dest:
                before = pltpu.roll(edge[dest - 1, plane, :, :LANE].astype(jnp.float32), NZ, 1)
            if dest < nodes - 1:
                after = pltpu.roll(edge[dest, plane, :, LANE:].astype(jnp.float32), NZ, 1)
            ends_out[dest, plane] = jnp.where(wide_lower, before, after).astype(jnp.bfloat16)
    for turn in range(1, nodes):
        ends_copy(turn).start()
    ends[me] = ends_out[me]
    lax.fori_loop(1, chunks, begin, 0)

    @pl.when(has_high)
    def _():
        kappa_copy(True).wait_send()
        kappa_copy(False).wait_recv()

    @pl.when(has_low)
    def _():
        kappa_copy(False).wait_send()
        kappa_copy(True).wait_recv()

    lane = lax.broadcasted_iota(jnp.int32, (8, LANE), 1)
    lower = lane < NZ
    zpos = lane % NZ
    inner = jnp.where(zpos == NZ - 1, 0.0, 0.5).astype(jnp.float32)
    rim = jnp.where(zpos == 0, 0.5, jnp.where(zpos == NZ - 1, 0.5, 0.0)).astype(jnp.float32)

    def cols(tile):
        return pl.ds(tile * LANE, LANE)

    def mine(tile):
        return pl.ds(pl.multiple_of((me * tiles + tile) * LANE, LANE), LANE)

    low_at = pl.ds(pl.multiple_of(jnp.maximum(me * tiles - 1, 0) * LANE, LANE), LANE)
    high_at = pl.ds(
        pl.multiple_of(jnp.minimum((me + 1) * tiles, nodes * tiles - 1) * LANE, LANE), LANE
    )
    for plane in range(2):
        kap = [kap_ref[plane, :, mine(t)] for t in range(tiles)]
        turned = [pltpu.roll(k, NZ, 1) for k in kap]
        before = pltpu.roll(kap_ref[plane, :, low_at], NZ, 1)
        after = pltpu.roll(kap_ref[plane, :, high_at], NZ, 1)
        before = before * jnp.where(me > 0, 1.0, 0.0)
        after = after * jnp.where(me < nodes - 1, 1.0, 0.0)
        for t in range(tiles):
            k = kap[t]
            up = jnp.where(lower, turned[t], turned[t + 1] if t + 1 < tiles else after)
            down = jnp.where(lower, turned[t - 1] if t else before, turned[t])
            coef[4 * plane, :, cols(t)] = inner * (k + pltpu.roll(k, LANE - 1, 1))
            coef[4 * plane + 1, :, cols(t)] = 0.5 * (k + up)
            coef[4 * plane + 2, :, cols(t)] = 0.5 * (k + down)
            coef[4 * plane + 3, :, cols(t)] = rim * k
    for t in range(tiles):
        low, high = (kap_ref[0, :, mine(t)], kap_ref[1, :, mine(t)])
        coef[8, :, cols(t)] = 0.5 * (low + kside[0, :, cols(t)])
        coef[9, :, cols(t)] = 0.5 * (low + high)
        coef[10, :, cols(t)] = 0.5 * (high + kside[1, :, cols(t)])

    def arrive(chunk):
        own_copy(chunk).wait()
        for turn in range(1, nodes):
            block_copy(chunk, turn).wait_recv()

        @pl.when(has_high)
        def _():
            side_copy(chunk, True).start()

        @pl.when(has_low)
        def _():
            side_copy(chunk, False).start()

    lower3 = lax.broadcasted_iota(jnp.int32, (ROWS // 8, 8, LANE), 2) < NZ

    def apply(chunk):
        @pl.when(has_high)
        def _():
            side_copy(chunk, False).wait_recv()

        @pl.when(has_low)
        def _():
            side_copy(chunk, True).wait_recv()

        rows = pl.ds(chunk * ROWS, ROWS)

        def one(node, carry):
            def wide(value):
                return value.astype(jnp.float32).reshape(ROWS // 8, 8, LANE)

            def load(plane, tile):
                return wide(held[node, plane, rows, cols(tile)])

            sides = [wide(ends[node, plane, rows, :]) for plane in range(2)]
            now = [load(plane, 0) for plane in range(2)]
            turned = [pltpu.roll(v, NZ, 2) for v in now]
            last = list(sides)
            for t in range(tiles):
                if t + 1 < tiles:
                    later = [load(plane, t + 1) for plane in range(2)]
                    coming = [pltpu.roll(v, NZ, 2) for v in later]
                else:
                    later, coming = (None, list(sides))
                mid = coef[9, :, cols(t)] * (now[0] - now[1])
                beside = [wide(side[p, node, rows, cols(t)]) for p in range(2)]
                for plane in range(2):
                    v = now[plane]
                    up = jnp.where(lower3, turned[plane], coming[plane])
                    down = jnp.where(lower3, last[plane], turned[plane])
                    flux = coef[4 * plane, :, cols(t)] * (v - pltpu.roll(v, LANE - 1, 2))
                    total = flux - pltpu.roll(flux, 1, 2)
                    total = total + coef[4 * plane + 3, :, cols(t)] * v
                    total = total + coef[4 * plane + 1, :, cols(t)] * (v - up)
                    total = total + coef[4 * plane + 2, :, cols(t)] * (v - down)
                    total = total + coef[8 + 2 * plane, :, cols(t)] * (v - beside[plane])
                    total = total - mid if plane else total + mid
                    image[node, plane, rows, cols(t)] = total.reshape(ROWS, LANE).astype(
                        jnp.bfloat16
                    )
                last, turned, now = (turned, coming, later)
            return carry

        lax.fori_loop(0, nodes, one, 0)

    arrive(0)
    for turn in range(1, nodes):
        ends_copy(turn).wait_recv()

    def step(chunk, carry):
        arrive(chunk)
        apply(chunk - 1)
        return carry

    lax.fori_loop(1, chunks, step, 0)
    apply(chunks - 1)

    order = nodes * snap_rows
    half = snap_rows // 2
    core = lax.rem(at, 2)
    partner = at + 1 - 2 * core
    layer = at // 2
    kept = pl.ds(pl.multiple_of(core * half, half), half)
    given = pl.ds(pl.multiple_of((1 - core) * half, half), half)

    def product(block):
        def part(index, carry):
            tile = jnp.zeros((snap_rows, 2 * snap_rows), jnp.float32)
            for plane in range(2):
                right = held[pl.ds(index * 2, 2), plane].reshape(2 * snap_rows, length)
                tile = tile + lax.dot_general(
                    image[block, plane], right, (((1,), (1,)), ((), ())),
                    preferred_element_type=jnp.float32,
                )
            place = pl.ds(pl.multiple_of(index * 2 * snap_rows, 2 * snap_rows), 2 * snap_rows)
            gram[block, :, place] = tile
            return carry

        lax.fori_loop(0, nodes // 2, part, 0)

    def first_copy(turn):
        block = lax.rem(me + turn, nodes)
        return pltpu.make_async_remote_copy(
            src_ref=gram.at[block, given],
            dst_ref=first.at[turn],
            send_sem=send1.at[turn],
            recv_sem=recv1.at[turn],
            device_id={"space": partner},
            device_id_type=MESH,
        )

    def second_copy(turn):
        return pltpu.make_async_remote_copy(
            src_ref=first.at[turn],
            dst_ref=second.at[turn - 1],
            send_sem=send2.at[turn - 1],
            recv_sem=recv2.at[turn - 1],
            device_id={"node": lax.rem(me + turn, nodes)},
            device_id_type=MESH,
        )

    def third_copy(turn):
        dest = lax.rem(layer + turn, layers)
        return pltpu.make_async_remote_copy(
            src_ref=first.at[0, :, pl.ds(pl.multiple_of(dest * LANE, LANE), LANE)],
            dst_ref=third.at[turn - 1],
            send_sem=send3.at[turn - 1],
            recv_sem=recv3.at[turn - 1],
            device_id={"space": lax.rem(at + 2 * turn, spaces)},
            device_id_type=MESH,
        )

    fourth_copy = pltpu.make_async_remote_copy(
        src_ref=fourth.at[0],
        dst_ref=fourth.at[1],
        send_sem=send4,
        recv_sem=recv4,
        device_id={"space": partner},
        device_id_type=MESH,
    )

    turns = list(range(1, nodes)) + [0]

    def paired(turn):
        first_copy(turn).wait_recv()
        block = lax.rem(me + turn, nodes)
        first[turn] = first[turn] + gram[block, kept]
        if turn:
            second_copy(turn).start()

    if summed:
        for place, turn in enumerate(turns):
            product(lax.rem(me + turn, nodes))
            first_copy(turn).start()
            if place:
                paired(turns[place - 1])
        paired(0)
        for turn in range(1, nodes):
            second_copy(turn).wait_recv()
            first[0] = first[0] + second[turn - 1]
        for turn in range(1, layers):
            third_copy(turn).start()
        own = first[0, :, pl.ds(pl.multiple_of(layer * LANE, LANE), LANE)]
        for turn in range(1, layers):
            third_copy(turn).wait_recv()
            own = own + third[turn - 1]
        fourth[0] = own * scale
        fourth_copy.start()
        fourth_copy.wait()
        width = LANE // 2

        def taken(value):
            return jnp.where(core == 0, value[:, :width], value[:, width:])

        out_ref[kept] = taken(fourth[0])
        out_ref[given] = taken(fourth[1])
        for turn in range(nodes):
            first_copy(turn).wait_send()
        for turn in range(1, nodes):
            second_copy(turn).wait_send()
        for turn in range(1, layers):
            third_copy(turn).wait_send()
    else:
        for block in range(nodes):
            product(block)
            out_ref[block * snap_rows : (block + 1) * snap_rows] = gram[block]
    for turn in range(1, nodes):
        ends_copy(turn).wait_send()

    def finish(chunk, carry):
        for turn in range(1, nodes):
            block_copy(chunk, turn).wait_send()

        @pl.when(has_high)
        def _():
            side_copy(chunk, True).wait_send()

        @pl.when(has_low)
        def _():
            side_copy(chunk, False).wait_send()

        return carry

    lax.fori_loop(0, chunks, finish, 0)


def per_device(snapshots, kappa):
    snap_rows, planes, width = snapshots.shape
    nodes, spaces = (lax.axis_size("node"), lax.axis_size("space"))
    length = width // nodes
    chunks = snap_rows // ROWS
    order = nodes * snap_rows
    half = snap_rows // 2
    scale = 1.0 / math.sqrt(planes * spaces * NY * NZ)
    summed = order // spaces == LANE // 2
    layers = spaces // 2
    shape = (snap_rows, order // spaces) if summed else (order, order)
    result = pl.pallas_call(
        functools.partial(gram_kernel, nodes, spaces, scale),
        out_shape=jax.ShapeDtypeStruct(shape, jnp.float32),
        in_specs=[
            pl.BlockSpec(memory_space=pl.ANY),
            pl.BlockSpec(memory_space=pltpu.VMEM),
        ],
        out_specs=pl.BlockSpec(memory_space=pltpu.VMEM),
        scratch_shapes=[
            pltpu.VMEM((nodes, planes, snap_rows, length), jnp.bfloat16),
            pltpu.VMEM((nodes, planes, snap_rows, LANE), jnp.bfloat16),
            pltpu.VMEM((nodes, planes, snap_rows, LANE), jnp.bfloat16),
            pltpu.VMEM((nodes - 1, planes, snap_rows, 2 * LANE), jnp.bfloat16),
            pltpu.VMEM((2, nodes, snap_rows, length), jnp.bfloat16),
            pltpu.VMEM((2, 8, length), jnp.float32),
            pltpu.VMEM((11, 8, length), jnp.float32),
            pltpu.VMEM((nodes, planes, snap_rows, length), jnp.bfloat16),
            pltpu.VMEM((nodes, snap_rows, order), jnp.float32),
            pltpu.VMEM((nodes, half, order), jnp.float32),
            pltpu.VMEM((nodes - 1, half, order), jnp.float32),
            pltpu.VMEM((layers - 1, half, LANE), jnp.float32),
            pltpu.VMEM((2, half, LANE), jnp.float32),
            pltpu.SemaphoreType.DMA((chunks,)),
            pltpu.SemaphoreType.DMA((nodes - 1,)),
            pltpu.SemaphoreType.DMA((nodes - 1, chunks)),
            pltpu.SemaphoreType.DMA((nodes - 1, chunks)),
            pltpu.SemaphoreType.DMA((nodes - 1,)),
            pltpu.SemaphoreType.DMA((nodes - 1,)),
            pltpu.SemaphoreType.DMA((2, chunks)),
            pltpu.SemaphoreType.DMA((2, chunks)),
            pltpu.SemaphoreType.DMA((2,)),
            pltpu.SemaphoreType.DMA((2,)),
            pltpu.SemaphoreType.DMA((nodes,)),
            pltpu.SemaphoreType.DMA((nodes,)),
            pltpu.SemaphoreType.DMA((nodes - 1,)),
            pltpu.SemaphoreType.DMA((nodes - 1,)),
            pltpu.SemaphoreType.DMA((layers - 1,)),
            pltpu.SemaphoreType.DMA((layers - 1,)),
            pltpu.SemaphoreType.DMA,
            pltpu.SemaphoreType.DMA,
        ],
        compiler_params=pltpu.CompilerParams(
            collective_id=0, has_side_effects=True, vmem_limit_bytes=48 * 1024 * 1024
        ),
        name="gram_sums",
    )(
        jnp.transpose(snapshots, (1, 0, 2)),
        jnp.broadcast_to(kappa.astype(jnp.float32)[:, None], (planes, 8, width)),
    )
    if summed:
        return result
    mine = lax.psum_scatter(result, "node", scatter_dimension=0, tiled=True)
    return lax.psum_scatter(mine, "space", scatter_dimension=1, tiled=True) * scale


def solution(mesh):
    placed = (P("node", "space", None), P("space", None))
    return jax.shard_map(
        per_device, mesh=mesh, in_specs=placed, out_specs=P("node", "space"), check_vma=False
    )
```

```python
import functools
import math

import jax
import jax.numpy as jnp
from jax import lax
from jax.experimental import pallas as pl
from jax.experimental.pallas import tpu as pltpu
from jax.sharding import PartitionSpec as P

NY = 128
NZ = 64
LANE = 128
ROWS = 16
MESH = pl.DeviceIdType.MESH


def gram_kernel(
    nodes, spaces, scale, snap_ref, kap_ref, out_ref,
    held, ends, ends_out, edge, side, kside, coef, image, gram, first, second, third,
    own_sem, edge_sem, send_sem, recv_sem, esend, erecv, hsend, hrecv, ksend, krecv,
    send1, recv1, send2, recv2, send3, recv3,
):
    me = lax.axis_index("node")
    at = lax.axis_index("space")
    snap_rows = snap_ref.shape[1]
    length = snap_ref.shape[2] // nodes
    tiles = length // LANE
    chunks = snap_rows // ROWS
    has_low = at > 0
    has_high = at < spaces - 1
    summed = out_ref.shape[0] != nodes * snap_rows
    layers = spaces // 2 if summed else 1

    def edge_copy(index):
        return pltpu.make_async_copy(
            snap_ref.at[:, :, pl.ds((index + 1) * length - LANE, 2 * LANE)],
            edge.at[index],
            edge_sem.at[index],
        )

    for index in range(nodes - 1):
        edge_copy(index).start()

    barrier = pltpu.get_barrier_semaphore()
    for turn in range(1, nodes):
        pl.semaphore_signal(
            barrier, inc=1, device_id={"node": lax.rem(me + turn, nodes)}, device_id_type=MESH
        )
    for turn in range(1, layers):
        pl.semaphore_signal(
            barrier,
            inc=1,
            device_id={"space": lax.rem(at + 2 * turn, spaces)},
            device_id_type=MESH,
        )

    @pl.when(has_low)
    def _():
        pl.semaphore_signal(barrier, inc=1, device_id={"space": at - 1}, device_id_type=MESH)

    @pl.when(has_high)
    def _():
        pl.semaphore_signal(barrier, inc=1, device_id={"space": at + 1}, device_id_type=MESH)

    @pl.when(jnp.logical_not(has_low))
    def _():
        side[0] = jnp.zeros(side.shape[1:], side.dtype)
        kside[0] = jnp.zeros(kside.shape[1:], kside.dtype)

    @pl.when(jnp.logical_not(has_high))
    def _():
        side[1] = jnp.zeros(side.shape[1:], side.dtype)
        kside[1] = jnp.zeros(kside.shape[1:], kside.dtype)

    both = jnp.logical_and(has_low, has_high)

    @pl.when(both)
    def _():
        pl.semaphore_wait(barrier, nodes + layers)

    @pl.when(jnp.logical_not(both))
    def _():
        pl.semaphore_wait(barrier, nodes + layers - 1)

    def own_copy(chunk):
        rows = pl.ds(chunk * ROWS, ROWS)
        return pltpu.make_async_copy(
            snap_ref.at[:, rows, pl.ds(pl.multiple_of(me * length, LANE), length)],
            held.at[me, :, rows],
            own_sem.at[chunk],
        )

    def block_copy(chunk, turn):
        rows = pl.ds(chunk * ROWS, ROWS)
        peer = lax.rem(me + turn, nodes)
        return pltpu.make_async_remote_copy(
            src_ref=snap_ref.at[:, rows, pl.ds(pl.multiple_of(peer * length, LANE), length)],
            dst_ref=held.at[me, :, rows],
            send_sem=send_sem.at[turn - 1, chunk],
            recv_sem=recv_sem.at[turn - 1, chunk],
            device_id={"node": peer},
            device_id_type=MESH,
        )

    def side_copy(chunk, high):
        rows = pl.ds(chunk * ROWS, ROWS)
        return pltpu.make_async_remote_copy(
            src_ref=held.at[:, 1 if high else 0, rows],
            dst_ref=side.at[0 if high else 1, :, rows],
            send_sem=hsend.at[0 if high else 1, chunk],
            recv_sem=hrecv.at[0 if high else 1, chunk],
            device_id={"space": at + 1 if high else at - 1},
            device_id_type=MESH,
        )

    def kappa_copy(high):
        return pltpu.make_async_remote_copy(
            src_ref=kap_ref.at[1 if high else 0, :, pl.ds(pl.multiple_of(me * length, LANE), length)],
            dst_ref=kside.at[0 if high else 1],
            send_sem=ksend.at[0 if high else 1],
            recv_sem=krecv.at[0 if high else 1],
            device_id={"space": at + 1 if high else at - 1},
            device_id_type=MESH,
        )

    def ends_copy(turn):
        peer = lax.rem(me + turn, nodes)
        return pltpu.make_async_remote_copy(
            src_ref=ends_out.at[peer],
            dst_ref=ends.at[me],
            send_sem=esend.at[turn - 1],
            recv_sem=erecv.at[turn - 1],
            device_id={"node": peer},
            device_id_type=MESH,
        )

    @pl.when(has_high)
    def _():
        kappa_copy(True).start()

    @pl.when(has_low)
    def _():
        kappa_copy(False).start()

    def begin(chunk, carry):
        own_copy(chunk).start()
        for turn in range(1, nodes):
            block_copy(chunk, turn).start()
        return carry

    begin(0, 0)
    for index in range(nodes - 1):
        edge_copy(index).wait()

    wide_lower = lax.broadcasted_iota(jnp.int32, (snap_rows, LANE), 1) < NZ
    for dest in range(nodes):
        for plane in range(2):
            before = after = jnp.zeros((snap_rows, LANE), jnp.float32)
            if dest:
                before = pltpu.roll(edge[dest - 1, plane, :, :LANE].astype(jnp.float32), NZ, 1)
            if dest < nodes - 1:
                after = pltpu.roll(edge[dest, plane, :, LANE:].astype(jnp.float32), NZ, 1)
            ends_out[dest, plane] = jnp.where(wide_lower, before, after).astype(jnp.bfloat16)
    for turn in range(1, nodes):
        ends_copy(turn).start()
    ends[me] = ends_out[me]
    lax.fori_loop(1, chunks, begin, 0)

    @pl.when(has_high)
    def _():
        kappa_copy(True).wait_send()
        kappa_copy(False).wait_recv()

    @pl.when(has_low)
    def _():
        kappa_copy(False).wait_send()
        kappa_copy(True).wait_recv()

    lane = lax.broadcasted_iota(jnp.int32, (8, LANE), 1)
    lower = lane < NZ
    zpos = lane % NZ
    inner = jnp.where(zpos == NZ - 1, 0.0, 0.5).astype(jnp.float32)
    rim = jnp.where(zpos == 0, 0.5, jnp.where(zpos == NZ - 1, 0.5, 0.0)).astype(jnp.float32)

    def cols(tile):
        return pl.ds(tile * LANE, LANE)

    def mine(tile):
        return pl.ds(pl.multiple_of((me * tiles + tile) * LANE, LANE), LANE)

    low_at = pl.ds(pl.multiple_of(jnp.maximum(me * tiles - 1, 0) * LANE, LANE), LANE)
    high_at = pl.ds(
        pl.multiple_of(jnp.minimum((me + 1) * tiles, nodes * tiles - 1) * LANE, LANE), LANE
    )
    for plane in range(2):
        kap = [kap_ref[plane, :, mine(t)] for t in range(tiles)]
        turned = [pltpu.roll(k, NZ, 1) for k in kap]
        before = pltpu.roll(kap_ref[plane, :, low_at], NZ, 1)
        after = pltpu.roll(kap_ref[plane, :, high_at], NZ, 1)
        before = before * jnp.where(me > 0, 1.0, 0.0)
        after = after * jnp.where(me < nodes - 1, 1.0, 0.0)
        for t in range(tiles):
            k = kap[t]
            up = jnp.where(lower, turned[t], turned[t + 1] if t + 1 < tiles else after)
            down = jnp.where(lower, turned[t - 1] if t else before, turned[t])
            coef[4 * plane, :, cols(t)] = inner * (k + pltpu.roll(k, LANE - 1, 1))
            coef[4 * plane + 1, :, cols(t)] = 0.5 * (k + up)
            coef[4 * plane + 2, :, cols(t)] = 0.5 * (k + down)
            coef[4 * plane + 3, :, cols(t)] = rim * k
    for t in range(tiles):
        low, high = (kap_ref[0, :, mine(t)], kap_ref[1, :, mine(t)])
        coef[8, :, cols(t)] = 0.5 * (low + kside[0, :, cols(t)])
        coef[9, :, cols(t)] = 0.5 * (low + high)
        coef[10, :, cols(t)] = 0.5 * (high + kside[1, :, cols(t)])

    def arrive(chunk):
        own_copy(chunk).wait()
        for turn in range(1, nodes):
            block_copy(chunk, turn).wait_recv()

        @pl.when(has_high)
        def _():
            side_copy(chunk, True).start()

        @pl.when(has_low)
        def _():
            side_copy(chunk, False).start()

    lower3 = lax.broadcasted_iota(jnp.int32, (ROWS // 8, 8, LANE), 2) < NZ

    def apply(chunk):
        @pl.when(has_high)
        def _():
            side_copy(chunk, False).wait_recv()

        @pl.when(has_low)
        def _():
            side_copy(chunk, True).wait_recv()

        rows = pl.ds(chunk * ROWS, ROWS)

        def one(node, carry):
            def wide(value):
                return value.astype(jnp.float32).reshape(ROWS // 8, 8, LANE)

            def load(plane, tile):
                return wide(held[node, plane, rows, cols(tile)])

            sides = [wide(ends[node, plane, rows, :]) for plane in range(2)]
            now = [load(plane, 0) for plane in range(2)]
            turned = [pltpu.roll(v, NZ, 2) for v in now]
            last = list(sides)
            for t in range(tiles):
                if t + 1 < tiles:
                    later = [load(plane, t + 1) for plane in range(2)]
                    coming = [pltpu.roll(v, NZ, 2) for v in later]
                else:
                    later, coming = (None, list(sides))
                mid = coef[9, :, cols(t)] * (now[0] - now[1])
                beside = [wide(side[p, node, rows, cols(t)]) for p in range(2)]
                for plane in range(2):
                    v = now[plane]
                    up = jnp.where(lower3, turned[plane], coming[plane])
                    down = jnp.where(lower3, last[plane], turned[plane])
                    flux = coef[4 * plane, :, cols(t)] * (v - pltpu.roll(v, LANE - 1, 2))
                    total = flux - pltpu.roll(flux, 1, 2)
                    total = total + coef[4 * plane + 3, :, cols(t)] * v
                    total = total + coef[4 * plane + 1, :, cols(t)] * (v - up)
                    total = total + coef[4 * plane + 2, :, cols(t)] * (v - down)
                    total = total + coef[8 + 2 * plane, :, cols(t)] * (v - beside[plane])
                    total = total - mid if plane else total + mid
                    image[node, plane, rows, cols(t)] = total.reshape(ROWS, LANE).astype(
                        jnp.bfloat16
                    )
                last, turned, now = (turned, coming, later)
            return carry

        lax.fori_loop(0, nodes, one, 0)

    arrive(0)
    for turn in range(1, nodes):
        ends_copy(turn).wait_recv()

    def step(chunk, carry):
        arrive(chunk)
        apply(chunk - 1)
        return carry

    lax.fori_loop(1, chunks, step, 0)
    apply(chunks - 1)

    order = nodes * snap_rows
    core = lax.rem(at, 2)
    partner = at + 1 - 2 * core
    layer = at // 2

    def product(pair):
        tile = jnp.zeros((order, 2 * snap_rows), jnp.float32)
        for plane in range(2):
            left = held[:, plane].reshape(order, length)
            right = image[2 * pair : 2 * pair + 2, plane].reshape(2 * snap_rows, length)
            tile = tile + lax.dot_general(
                left, right, (((1,), (1,)), ((), ())), preferred_element_type=jnp.float32
            )
        for index in range(2):
            part = tile[:, index * snap_rows : (index + 1) * snap_rows]
            gram[2 * pair + index] = part.reshape(gram.shape[1:])

    for pair in range(nodes // 2):
        product(pair)

    def first_copy(turn):
        return pltpu.make_async_remote_copy(
            src_ref=gram.at[lax.rem(me + turn, nodes), :, 1 - core],
            dst_ref=first.at[turn],
            send_sem=send1.at[turn],
            recv_sem=recv1.at[turn],
            device_id={"space": partner},
            device_id_type=MESH,
        )

    def second_copy(turn):
        return pltpu.make_async_remote_copy(
            src_ref=first.at[turn],
            dst_ref=second.at[turn - 1],
            send_sem=send2.at[turn - 1],
            recv_sem=recv2.at[turn - 1],
            device_id={"node": lax.rem(me + turn, nodes)},
            device_id_type=MESH,
        )

    def third_copy(turn):
        return pltpu.make_async_remote_copy(
            src_ref=first.at[0, lax.rem(layer + turn, layers)],
            dst_ref=third.at[turn - 1],
            send_sem=send3.at[turn - 1],
            recv_sem=recv3.at[turn - 1],
            device_id={"space": lax.rem(at + 2 * turn, spaces)},
            device_id_type=MESH,
        )

    if summed:
        turns = list(range(1, nodes)) + [0]
        for turn in turns:
            first_copy(turn).start()
        for turn in turns:
            first_copy(turn).wait_recv()
            first[turn] = first[turn] + gram[lax.rem(me + turn, nodes), :, core]
            if turn:
                second_copy(turn).start()
        for turn in range(1, nodes):
            second_copy(turn).wait_recv()
        total = first[0]
        for turn in range(1, nodes):
            total = total + second[turn - 1]
        first[0] = total
        for turn in range(1, layers):
            third_copy(turn).start()
        own = first[0, layer]
        for turn in range(1, layers):
            third_copy(turn).wait_recv()
            own = own + third[turn - 1]
        out_ref[...] = own * scale
        for turn in range(nodes):
            first_copy(turn).wait_send()
        for turn in range(1, nodes):
            second_copy(turn).wait_send()
        for turn in range(1, layers):
            third_copy(turn).wait_send()
    else:
        for block in range(nodes):
            out_ref[block * snap_rows : (block + 1) * snap_rows] = gram[block].reshape(
                order, snap_rows
            ).T
    for turn in range(1, nodes):
        ends_copy(turn).wait_send()

    def finish(chunk, carry):
        for turn in range(1, nodes):
            block_copy(chunk, turn).wait_send()

        @pl.when(has_high)
        def _():
            side_copy(chunk, True).wait_send()

        @pl.when(has_low)
        def _():
            side_copy(chunk, False).wait_send()

        return carry

    lax.fori_loop(0, chunks, finish, 0)


def per_device(snapshots, kappa):
    snap_rows, planes, width = snapshots.shape
    nodes, spaces = (lax.axis_size("node"), lax.axis_size("space"))
    length = width // nodes
    chunks = snap_rows // ROWS
    order = nodes * snap_rows
    scale = 1.0 / math.sqrt(planes * spaces * NY * NZ)
    share = order // spaces
    summed = share % 8 == 0 and share * spaces == order and spaces % 2 == 0 and share >= 64
    layers = spaces // 2
    shape = (share, snap_rows) if summed else (order, order)
    blocks = (layers, 2, share) if summed else (1, 1, order)
    result = pl.pallas_call(
        functools.partial(gram_kernel, nodes, spaces, scale),
        out_shape=jax.ShapeDtypeStruct(shape, jnp.float32),
        in_specs=[
            pl.BlockSpec(memory_space=pl.ANY),
            pl.BlockSpec(memory_space=pltpu.VMEM),
        ],
        out_specs=pl.BlockSpec(memory_space=pltpu.VMEM),
        scratch_shapes=[
            pltpu.VMEM((nodes, planes, snap_rows, length), jnp.bfloat16),
            pltpu.VMEM((nodes, planes, snap_rows, LANE), jnp.bfloat16),
            pltpu.VMEM((nodes, planes, snap_rows, LANE), jnp.bfloat16),
            pltpu.VMEM((nodes - 1, planes, snap_rows, 2 * LANE), jnp.bfloat16),
            pltpu.VMEM((2, nodes, snap_rows, length), jnp.bfloat16),
            pltpu.VMEM((2, 8, length), jnp.float32),
            pltpu.VMEM((11, 8, length), jnp.float32),
            pltpu.VMEM((nodes, planes, snap_rows, length), jnp.bfloat16),
            pltpu.VMEM((nodes,) + blocks + (snap_rows,), jnp.float32),
            pltpu.VMEM((nodes, blocks[0], blocks[2], snap_rows), jnp.float32),
            pltpu.VMEM((nodes - 1, blocks[0], blocks[2], snap_rows), jnp.float32),
            pltpu.VMEM((layers - 1, blocks[2], snap_rows), jnp.float32),
            pltpu.SemaphoreType.DMA((chunks,)),
            pltpu.SemaphoreType.DMA((nodes - 1,)),
            pltpu.SemaphoreType.DMA((nodes - 1, chunks)),
            pltpu.SemaphoreType.DMA((nodes - 1, chunks)),
            pltpu.SemaphoreType.DMA((nodes - 1,)),
            pltpu.SemaphoreType.DMA((nodes - 1,)),
            pltpu.SemaphoreType.DMA((2, chunks)),
            pltpu.SemaphoreType.DMA((2, chunks)),
            pltpu.SemaphoreType.DMA((2,)),
            pltpu.SemaphoreType.DMA((2,)),
            pltpu.SemaphoreType.DMA((nodes,)),
            pltpu.SemaphoreType.DMA((nodes,)),
            pltpu.SemaphoreType.DMA((nodes - 1,)),
            pltpu.SemaphoreType.DMA((nodes - 1,)),
            pltpu.SemaphoreType.DMA((layers - 1,)),
            pltpu.SemaphoreType.DMA((layers - 1,)),
        ],
        compiler_params=pltpu.CompilerParams(
            collective_id=0, has_side_effects=True, vmem_limit_bytes=48 * 1024 * 1024
        ),
        name="gram_sums",
    )(
        jnp.transpose(snapshots, (1, 0, 2)),
        jnp.broadcast_to(kappa.astype(jnp.float32)[:, None], (planes, 8, width)),
    )
    if summed:
        return result.T
    mine = lax.psum_scatter(result, "node", scatter_dimension=0, tiled=True)
    return lax.psum_scatter(mine, "space", scatter_dimension=1, tiled=True) * scale


def solution(mesh):
    placed = (P("node", "space", None), P("space", None))
    return jax.shard_map(
        per_device, mesh=mesh, in_specs=placed, out_specs=P("node", "space"), check_vma=False
    )
```

```python
import functools
import math

import jax
import jax.numpy as jnp
from jax import lax
from jax.experimental import pallas as pl
from jax.experimental.pallas import tpu as pltpu
from jax.sharding import PartitionSpec as P

NY = 128
NZ = 64
LANE = 128
ROWS = 16
MESH = pl.DeviceIdType.MESH


def gram_kernel(
    nodes, spaces, scale, snap_ref, kap_ref, out_ref,
    raw, sent, held, side, kside, coef, image, gram, first, second, third,
    raw_sem, own_sem, send_sem, recv_sem, hsend, hrecv, ksend, krecv,
    send1, recv1, send2, recv2, send3, recv3,
):
    me = lax.axis_index("node")
    at = lax.axis_index("space")
    snap_rows = snap_ref.shape[0]
    length = snap_ref.shape[2] // nodes
    tiles = length // LANE
    chunks = snap_rows // ROWS
    has_low = at > 0
    has_high = at < spaces - 1
    summed = out_ref.shape[0] != nodes * snap_rows
    layers = spaces // 2 if summed else 1

    def raw_copy(chunk):
        rows = pl.ds(chunk * ROWS, ROWS)
        return pltpu.make_async_copy(snap_ref.at[rows], raw.at[rows], raw_sem.at[chunk])

    for chunk in range(chunks):
        raw_copy(chunk).start()

    low_rows = lax.broadcasted_iota(jnp.int32, (ROWS, LANE), 1) < NZ

    def spread(chunk):
        rows = pl.ds(pl.multiple_of(chunk * ROWS, ROWS), ROWS)
        raw_copy(chunk).wait()
        for plane in range(2):

            def turned_tile(first):
                value = raw[rows, plane, first : first + LANE].astype(jnp.float32)
                return pltpu.roll(value, NZ, 1)

            for dest in range(nodes):
                low, high = (dest * length, (dest + 1) * length)
                sent[dest, plane, rows, :length] = raw[rows, plane, low:high]
                before = after = jnp.zeros((ROWS, LANE), jnp.float32)
                if dest:
                    before = turned_tile(low - LANE)
                if dest < nodes - 1:
                    after = turned_tile(high)
                sent[dest, plane, rows, length:] = jnp.where(low_rows, before, after).astype(
                    jnp.bfloat16
                )

    spread(0)
    barrier = pltpu.get_barrier_semaphore()
    for turn in range(1, nodes):
        pl.semaphore_signal(
            barrier, inc=1, device_id={"node": lax.rem(me + turn, nodes)}, device_id_type=MESH
        )
    for turn in range(1, layers):
        pl.semaphore_signal(
            barrier,
            inc=1,
            device_id={"space": lax.rem(at + 2 * turn, spaces)},
            device_id_type=MESH,
        )

    @pl.when(has_low)
    def _():
        pl.semaphore_signal(barrier, inc=1, device_id={"space": at - 1}, device_id_type=MESH)

    @pl.when(has_high)
    def _():
        pl.semaphore_signal(barrier, inc=1, device_id={"space": at + 1}, device_id_type=MESH)

    @pl.when(jnp.logical_not(has_low))
    def _():
        side[0] = jnp.zeros(side.shape[1:], side.dtype)
        kside[0] = jnp.zeros(kside.shape[1:], kside.dtype)

    @pl.when(jnp.logical_not(has_high))
    def _():
        side[1] = jnp.zeros(side.shape[1:], side.dtype)
        kside[1] = jnp.zeros(kside.shape[1:], kside.dtype)

    both = jnp.logical_and(has_low, has_high)

    @pl.when(both)
    def _():
        pl.semaphore_wait(barrier, nodes + layers)

    @pl.when(jnp.logical_not(both))
    def _():
        pl.semaphore_wait(barrier, nodes + layers - 1)

    def own_copy(chunk):
        rows = pl.ds(chunk * ROWS, ROWS)
        return pltpu.make_async_copy(
            sent.at[me, :, rows],
            held.at[me, :, rows],
            own_sem.at[chunk],
        )

    def block_copy(chunk, turn):
        rows = pl.ds(chunk * ROWS, ROWS)
        peer = lax.rem(me + turn, nodes)
        return pltpu.make_async_remote_copy(
            src_ref=sent.at[peer, :, rows],
            dst_ref=held.at[me, :, rows],
            send_sem=send_sem.at[turn - 1, chunk],
            recv_sem=recv_sem.at[turn - 1, chunk],
            device_id={"node": peer},
            device_id_type=MESH,
        )

    def side_copy(chunk, high):
        rows = pl.ds(chunk * ROWS, ROWS)
        return pltpu.make_async_remote_copy(
            src_ref=held.at[:, 1 if high else 0, rows, pl.ds(0, length)],
            dst_ref=side.at[0 if high else 1, :, rows],
            send_sem=hsend.at[0 if high else 1, chunk],
            recv_sem=hrecv.at[0 if high else 1, chunk],
            device_id={"space": at + 1 if high else at - 1},
            device_id_type=MESH,
        )

    def kappa_copy(high):
        return pltpu.make_async_remote_copy(
            src_ref=kap_ref.at[1 if high else 0, :, pl.ds(pl.multiple_of(me * length, LANE), length)],
            dst_ref=kside.at[0 if high else 1],
            send_sem=ksend.at[0 if high else 1],
            recv_sem=krecv.at[0 if high else 1],
            device_id={"space": at + 1 if high else at - 1},
            device_id_type=MESH,
        )

    @pl.when(has_high)
    def _():
        kappa_copy(True).start()

    @pl.when(has_low)
    def _():
        kappa_copy(False).start()

    def begin(chunk, carry):
        own_copy(chunk).start()
        for turn in range(1, nodes):
            block_copy(chunk, turn).start()
        return carry

    begin(0, 0)

    def follow(chunk, carry):
        spread(chunk)
        return begin(chunk, carry)

    lax.fori_loop(1, chunks, follow, 0)

    @pl.when(has_high)
    def _():
        kappa_copy(True).wait_send()
        kappa_copy(False).wait_recv()

    @pl.when(has_low)
    def _():
        kappa_copy(False).wait_send()
        kappa_copy(True).wait_recv()

    lane = lax.broadcasted_iota(jnp.int32, (8, LANE), 1)
    lower = lane < NZ
    zpos = lane % NZ
    inner = jnp.where(zpos == NZ - 1, 0.0, 0.5).astype(jnp.float32)
    rim = jnp.where(zpos == 0, 0.5, jnp.where(zpos == NZ - 1, 0.5, 0.0)).astype(jnp.float32)

    def cols(tile):
        return pl.ds(tile * LANE, LANE)

    def mine(tile):
        return pl.ds(pl.multiple_of((me * tiles + tile) * LANE, LANE), LANE)

    low_at = pl.ds(pl.multiple_of(jnp.maximum(me * tiles - 1, 0) * LANE, LANE), LANE)
    high_at = pl.ds(
        pl.multiple_of(jnp.minimum((me + 1) * tiles, nodes * tiles - 1) * LANE, LANE), LANE
    )
    for plane in range(2):
        kap = [kap_ref[plane, :, mine(t)] for t in range(tiles)]
        turned = [pltpu.roll(k, NZ, 1) for k in kap]
        before = pltpu.roll(kap_ref[plane, :, low_at], NZ, 1)
        after = pltpu.roll(kap_ref[plane, :, high_at], NZ, 1)
        before = before * jnp.where(me > 0, 1.0, 0.0)
        after = after * jnp.where(me < nodes - 1, 1.0, 0.0)
        for t in range(tiles):
            k = kap[t]
            up = jnp.where(lower, turned[t], turned[t + 1] if t + 1 < tiles else after)
            down = jnp.where(lower, turned[t - 1] if t else before, turned[t])
            coef[4 * plane, :, cols(t)] = inner * (k + pltpu.roll(k, LANE - 1, 1))
            coef[4 * plane + 1, :, cols(t)] = 0.5 * (k + up)
            coef[4 * plane + 2, :, cols(t)] = 0.5 * (k + down)
            coef[4 * plane + 3, :, cols(t)] = rim * k
    for t in range(tiles):
        low, high = (kap_ref[0, :, mine(t)], kap_ref[1, :, mine(t)])
        coef[8, :, cols(t)] = 0.5 * (low + kside[0, :, cols(t)])
        coef[9, :, cols(t)] = 0.5 * (low + high)
        coef[10, :, cols(t)] = 0.5 * (high + kside[1, :, cols(t)])

    def arrive(chunk):
        own_copy(chunk).wait()
        for turn in range(1, nodes):
            block_copy(chunk, turn).wait_recv()

        @pl.when(has_high)
        def _():
            side_copy(chunk, True).start()

        @pl.when(has_low)
        def _():
            side_copy(chunk, False).start()

    lower3 = lax.broadcasted_iota(jnp.int32, (ROWS // 8, 8, LANE), 2) < NZ

    def apply(chunk):
        @pl.when(has_high)
        def _():
            side_copy(chunk, False).wait_recv()

        @pl.when(has_low)
        def _():
            side_copy(chunk, True).wait_recv()

        rows = pl.ds(chunk * ROWS, ROWS)

        def one(node, carry):
            def wide(value):
                return value.astype(jnp.float32).reshape(ROWS // 8, 8, LANE)

            def load(plane, tile):
                return wide(held[node, plane, rows, cols(tile)])

            sides = [load(plane, tiles) for plane in range(2)]
            now = [load(plane, 0) for plane in range(2)]
            turned = [pltpu.roll(v, NZ, 2) for v in now]
            last = list(sides)
            for t in range(tiles):
                if t + 1 < tiles:
                    later = [load(plane, t + 1) for plane in range(2)]
                    coming = [pltpu.roll(v, NZ, 2) for v in later]
                else:
                    later, coming = (None, list(sides))
                mid = coef[9, :, cols(t)] * (now[0] - now[1])
                beside = [wide(side[p, node, rows, cols(t)]) for p in range(2)]
                for plane in range(2):
                    v = now[plane]
                    up = jnp.where(lower3, turned[plane], coming[plane])
                    down = jnp.where(lower3, last[plane], turned[plane])
                    flux = coef[4 * plane, :, cols(t)] * (v - pltpu.roll(v, LANE - 1, 2))
                    total = flux - pltpu.roll(flux, 1, 2)
                    total = total + coef[4 * plane + 3, :, cols(t)] * v
                    total = total + coef[4 * plane + 1, :, cols(t)] * (v - up)
                    total = total + coef[4 * plane + 2, :, cols(t)] * (v - down)
                    total = total + coef[8 + 2 * plane, :, cols(t)] * (v - beside[plane])
                    total = total - mid if plane else total + mid
                    image[node, plane, rows, cols(t)] = total.reshape(ROWS, LANE).astype(
                        jnp.bfloat16
                    )
                last, turned, now = (turned, coming, later)
            return carry

        lax.fori_loop(0, nodes, one, 0)

    arrive(0)

    def step(chunk, carry):
        arrive(chunk)
        apply(chunk - 1)
        return carry

    lax.fori_loop(1, chunks, step, 0)
    apply(chunks - 1)

    order = nodes * snap_rows
    core = lax.rem(at, 2)
    partner = at + 1 - 2 * core
    layer = at // 2

    def product(pair):
        tile = jnp.zeros((order, 2 * snap_rows), jnp.float32)
        for plane in range(2):
            left = held[:, plane, :, :length].reshape(order, length)
            right = image[pl.ds(2 * pair, 2), plane].reshape(2 * snap_rows, length)
            tile = tile + lax.dot_general(
                left, right, (((1,), (1,)), ((), ())), preferred_element_type=jnp.float32
            )
        for index in range(2):
            part = tile[:, index * snap_rows : (index + 1) * snap_rows]
            gram[2 * pair + index] = part.reshape(gram.shape[1:])

    def first_copy(block):
        return pltpu.make_async_remote_copy(
            src_ref=gram.at[block, :, 1 - core],
            dst_ref=first.at[block],
            send_sem=send1.at[block],
            recv_sem=recv1.at[block],
            device_id={"space": partner},
            device_id_type=MESH,
        )

    def second_copy(turn):
        block = lax.rem(me + turn, nodes)
        return pltpu.make_async_remote_copy(
            src_ref=first.at[block],
            dst_ref=second.at[turn - 1],
            send_sem=send2.at[turn - 1],
            recv_sem=recv2.at[turn - 1],
            device_id={"node": block},
            device_id_type=MESH,
        )

    def third_copy(turn):
        return pltpu.make_async_remote_copy(
            src_ref=first.at[me, lax.rem(layer + turn, layers)],
            dst_ref=third.at[turn - 1],
            send_sem=send3.at[turn - 1],
            recv_sem=recv3.at[turn - 1],
            device_id={"space": lax.rem(at + 2 * turn, spaces)},
            device_id_type=MESH,
        )

    if summed:
        def joined(block):
            first_copy(block).wait_recv()
            first[block] = first[block] + gram[block, :, core]

        away = nodes // 2 - 1 - me // 2
        for index in range(nodes // 2):
            pair = lax.rem(away + index, nodes // 2)
            product(pair)
            for place in range(2):
                first_copy(2 * pair + place).start()
            if index == 0:
                ahead = pair
        for place in range(2):
            block = 2 * ahead + place
            joined(block)
            second_copy(lax.rem(block - me + nodes, nodes)).start()
        block = me + 1 - 2 * lax.rem(me, 2)
        joined(block)
        second_copy(lax.rem(block - me + nodes, nodes)).start()
        joined(me)
        for turn in range(1, nodes):
            second_copy(turn).wait_recv()
        total = first[me]
        for turn in range(1, nodes):
            total = total + second[turn - 1]
        first[me] = total
        for turn in range(1, layers):
            third_copy(turn).start()
        own = first[me, layer]
        for turn in range(1, layers):
            third_copy(turn).wait_recv()
            own = own + third[turn - 1]
        out_ref[...] = own * scale
        for turn in range(nodes):
            first_copy(turn).wait_send()
        for turn in range(1, nodes):
            second_copy(turn).wait_send()
        for turn in range(1, layers):
            third_copy(turn).wait_send()
    else:
        for pair in range(nodes // 2):
            product(pair)
        for block in range(nodes):
            out_ref[block * snap_rows : (block + 1) * snap_rows] = gram[block].reshape(
                order, snap_rows
            ).T

    def finish(chunk, carry):
        for turn in range(1, nodes):
            block_copy(chunk, turn).wait_send()

        @pl.when(has_high)
        def _():
            side_copy(chunk, True).wait_send()

        @pl.when(has_low)
        def _():
            side_copy(chunk, False).wait_send()

        return carry

    lax.fori_loop(0, chunks, finish, 0)


def per_device(snapshots, kappa):
    snap_rows, planes, width = snapshots.shape
    nodes, spaces = (lax.axis_size("node"), lax.axis_size("space"))
    length = width // nodes
    chunks = snap_rows // ROWS
    order = nodes * snap_rows
    scale = 1.0 / math.sqrt(planes * spaces * NY * NZ)
    share = order // spaces
    summed = share % 8 == 0 and share * spaces == order and spaces % 2 == 0 and share >= 64
    layers = spaces // 2
    shape = (share, snap_rows) if summed else (order, order)
    blocks = (layers, 2, share) if summed else (1, 1, order)
    result = pl.pallas_call(
        functools.partial(gram_kernel, nodes, spaces, scale),
        out_shape=jax.ShapeDtypeStruct(shape, jnp.float32),
        in_specs=[
            pl.BlockSpec(memory_space=pl.ANY),
            pl.BlockSpec(memory_space=pltpu.VMEM),
        ],
        out_specs=pl.BlockSpec(memory_space=pltpu.VMEM),
        scratch_shapes=[
            pltpu.VMEM((snap_rows, planes, width), jnp.bfloat16),
            pltpu.VMEM((nodes, planes, snap_rows, length + LANE), jnp.bfloat16),
            pltpu.VMEM((nodes, planes, snap_rows, length + LANE), jnp.bfloat16),
            pltpu.VMEM((2, nodes, snap_rows, length), jnp.bfloat16),
            pltpu.VMEM((2, 8, length), jnp.float32),
            pltpu.VMEM((11, 8, length), jnp.float32),
            pltpu.VMEM((nodes, planes, snap_rows, length), jnp.bfloat16),
            pltpu.VMEM((nodes,) + blocks + (snap_rows,), jnp.float32),
            pltpu.VMEM((nodes, blocks[0], blocks[2], snap_rows), jnp.float32),
            pltpu.VMEM((nodes - 1, blocks[0], blocks[2], snap_rows), jnp.float32),
            pltpu.VMEM((layers - 1, blocks[2], snap_rows), jnp.float32),
            pltpu.SemaphoreType.DMA((chunks,)),
            pltpu.SemaphoreType.DMA((chunks,)),
            pltpu.SemaphoreType.DMA((nodes - 1, chunks)),
            pltpu.SemaphoreType.DMA((nodes - 1, chunks)),
            pltpu.SemaphoreType.DMA((2, chunks)),
            pltpu.SemaphoreType.DMA((2, chunks)),
            pltpu.SemaphoreType.DMA((2,)),
            pltpu.SemaphoreType.DMA((2,)),
            pltpu.SemaphoreType.DMA((nodes,)),
            pltpu.SemaphoreType.DMA((nodes,)),
            pltpu.SemaphoreType.DMA((nodes - 1,)),
            pltpu.SemaphoreType.DMA((nodes - 1,)),
            pltpu.SemaphoreType.DMA((layers - 1,)),
            pltpu.SemaphoreType.DMA((layers - 1,)),
        ],
        compiler_params=pltpu.CompilerParams(
            collective_id=0, has_side_effects=True, vmem_limit_bytes=60 * 1024 * 1024
        ),
        name="gram_sums",
    )(
        snapshots,
        jnp.broadcast_to(kappa.astype(jnp.float32)[:, None], (planes, 8, width)),
    )
    if summed:
        return result.T
    mine = lax.psum_scatter(result, "node", scatter_dimension=0, tiled=True)
    return lax.psum_scatter(mine, "space", scatter_dimension=1, tiled=True) * scale


def solution(mesh):
    placed = (P("node", "space", None), P("space", None))
    return jax.shard_map(
        per_device, mesh=mesh, in_specs=placed, out_specs=P("node", "space"), check_vma=False
    )
```

```python
import functools
import math

import jax
import jax.numpy as jnp
from jax import lax
from jax.experimental import pallas as pl
from jax.experimental.pallas import tpu as pltpu
from jax.sharding import PartitionSpec as P

NY = 128
NZ = 64
LANE = 128
ROWS = 16
MESH = pl.DeviceIdType.MESH


def gram_kernel(
    nodes, spaces, scale, snap_ref, kap_ref, out_ref,
    raw, sent, held, side, kown, kside, coef, image, gram, first, second, third, late, cross,
    raw_sem, own_sem, send_sem, recv_sem, hsend, hrecv, ksend, krecv,
    send1, recv1, send2, recv2, send3, recv3, send4, recv4, send5, recv5,
):
    me = lax.axis_index("node")
    at = lax.axis_index("space")
    snap_rows = snap_ref.shape[0]
    length = snap_ref.shape[2] // nodes
    tiles = length // LANE
    chunks = snap_rows // ROWS
    has_low = at > 0
    has_high = at < spaces - 1
    summed = out_ref.shape[0] != nodes * snap_rows
    layers = spaces // 2 if summed else 1

    def raw_copy(chunk):
        rows = pl.ds(chunk * ROWS, ROWS)
        return pltpu.make_async_copy(snap_ref.at[rows], raw.at[rows], raw_sem.at[chunk])

    for chunk in range(chunks):
        raw_copy(chunk).start()

    low_rows = lax.broadcasted_iota(jnp.int32, (ROWS, LANE), 1) < NZ

    def spread(chunk):
        rows = pl.ds(pl.multiple_of(chunk * ROWS, ROWS), ROWS)
        raw_copy(chunk).wait()
        for plane in range(2):

            def turned_tile(first):
                value = raw[rows, plane, first : first + LANE].astype(jnp.float32)
                return pltpu.roll(value, NZ, 1)

            for dest in range(nodes):
                low, high = (dest * length, (dest + 1) * length)
                sent[dest, plane, rows, :length] = raw[rows, plane, low:high]
                before = after = jnp.zeros((ROWS, LANE), jnp.float32)
                if dest:
                    before = turned_tile(low - LANE)
                if dest < nodes - 1:
                    after = turned_tile(high)
                sent[dest, plane, rows, length:] = jnp.where(low_rows, before, after).astype(
                    jnp.bfloat16
                )

    spread(0)
    for plane in range(2):
        values = kap_ref[plane : plane + 1, pl.ds(pl.multiple_of(me * length, LANE), length)]
        kown[plane] = jnp.broadcast_to(values.astype(jnp.float32), (8, length))
    barrier = pltpu.get_barrier_semaphore()
    for turn in range(1, nodes):
        pl.semaphore_signal(
            barrier, inc=1, device_id={"node": lax.rem(me + turn, nodes)}, device_id_type=MESH
        )
    for turn in range(1, layers):
        pl.semaphore_signal(
            barrier,
            inc=1,
            device_id={"space": lax.rem(at + 2 * turn, spaces)},
            device_id_type=MESH,
        )

    @pl.when(has_low)
    def _():
        pl.semaphore_signal(barrier, inc=1, device_id={"space": at - 1}, device_id_type=MESH)

    @pl.when(has_high)
    def _():
        pl.semaphore_signal(barrier, inc=1, device_id={"space": at + 1}, device_id_type=MESH)

    @pl.when(jnp.logical_not(has_low))
    def _():
        side[0] = jnp.zeros(side.shape[1:], side.dtype)
        kside[0] = jnp.zeros(kside.shape[1:], kside.dtype)

    @pl.when(jnp.logical_not(has_high))
    def _():
        side[1] = jnp.zeros(side.shape[1:], side.dtype)
        kside[1] = jnp.zeros(kside.shape[1:], kside.dtype)

    both = jnp.logical_and(has_low, has_high)

    @pl.when(both)
    def _():
        pl.semaphore_wait(barrier, nodes + layers)

    @pl.when(jnp.logical_not(both))
    def _():
        pl.semaphore_wait(barrier, nodes + layers - 1)

    def own_copy(chunk):
        rows = pl.ds(chunk * ROWS, ROWS)
        return pltpu.make_async_copy(
            sent.at[me, :, rows],
            held.at[me, :, rows],
            own_sem.at[chunk],
        )

    def block_copy(chunk, turn):
        rows = pl.ds(chunk * ROWS, ROWS)
        peer = lax.rem(me + turn, nodes)
        return pltpu.make_async_remote_copy(
            src_ref=sent.at[peer, :, rows],
            dst_ref=held.at[me, :, rows],
            send_sem=send_sem.at[turn - 1, chunk],
            recv_sem=recv_sem.at[turn - 1, chunk],
            device_id={"node": peer},
            device_id_type=MESH,
        )

    def side_copy(chunk, high):
        rows = pl.ds(chunk * ROWS, ROWS)
        return pltpu.make_async_remote_copy(
            src_ref=held.at[:, 1 if high else 0, rows, pl.ds(0, length)],
            dst_ref=side.at[0 if high else 1, :, rows],
            send_sem=hsend.at[0 if high else 1, chunk],
            recv_sem=hrecv.at[0 if high else 1, chunk],
            device_id={"space": at + 1 if high else at - 1},
            device_id_type=MESH,
        )

    def kappa_copy(high):
        return pltpu.make_async_remote_copy(
            src_ref=kown.at[1 if high else 0],
            dst_ref=kside.at[0 if high else 1],
            send_sem=ksend.at[0 if high else 1],
            recv_sem=krecv.at[0 if high else 1],
            device_id={"space": at + 1 if high else at - 1},
            device_id_type=MESH,
        )

    @pl.when(has_high)
    def _():
        kappa_copy(True).start()

    @pl.when(has_low)
    def _():
        kappa_copy(False).start()

    def begin(chunk, carry):
        own_copy(chunk).start()
        for turn in range(1, nodes):
            block_copy(chunk, turn).start()
        return carry

    begin(0, 0)

    def follow(chunk, carry):
        spread(chunk)
        return begin(chunk, carry)

    lax.fori_loop(1, chunks, follow, 0)

    @pl.when(has_high)
    def _():
        kappa_copy(True).wait_send()
        kappa_copy(False).wait_recv()

    @pl.when(has_low)
    def _():
        kappa_copy(False).wait_send()
        kappa_copy(True).wait_recv()

    lane = lax.broadcasted_iota(jnp.int32, (8, LANE), 1)
    lower = lane < NZ
    zpos = lane % NZ
    inner = jnp.where(zpos == NZ - 1, 0.0, 0.5).astype(jnp.float32)
    rim = jnp.where(zpos == 0, 0.5, jnp.where(zpos == NZ - 1, 0.5, 0.0)).astype(jnp.float32)

    def cols(tile):
        return pl.ds(tile * LANE, LANE)

    low_at = pl.ds(pl.multiple_of(jnp.maximum(me * tiles - 1, 0) * LANE, LANE), LANE)
    high_at = pl.ds(
        pl.multiple_of(jnp.minimum((me + 1) * tiles, nodes * tiles - 1) * LANE, LANE), LANE
    )
    for plane in range(2):

        def beyond(place):
            value = kap_ref[plane : plane + 1, place].astype(jnp.float32)
            return pltpu.roll(jnp.broadcast_to(value, (8, LANE)), NZ, 1)

        kap = [kown[plane, :, cols(t)] for t in range(tiles)]
        turned = [pltpu.roll(k, NZ, 1) for k in kap]
        before = beyond(low_at)
        after = beyond(high_at)
        before = before * jnp.where(me > 0, 1.0, 0.0)
        after = after * jnp.where(me < nodes - 1, 1.0, 0.0)
        for t in range(tiles):
            k = kap[t]
            up = jnp.where(lower, turned[t], turned[t + 1] if t + 1 < tiles else after)
            down = jnp.where(lower, turned[t - 1] if t else before, turned[t])
            coef[4 * plane, :, cols(t)] = inner * (k + pltpu.roll(k, LANE - 1, 1))
            coef[4 * plane + 1, :, cols(t)] = 0.5 * (k + up)
            coef[4 * plane + 2, :, cols(t)] = 0.5 * (k + down)
            coef[4 * plane + 3, :, cols(t)] = rim * k
    for t in range(tiles):
        low, high = (kown[0, :, cols(t)], kown[1, :, cols(t)])
        coef[8, :, cols(t)] = 0.5 * (low + kside[0, :, cols(t)])
        coef[9, :, cols(t)] = 0.5 * (low + high)
        coef[10, :, cols(t)] = 0.5 * (high + kside[1, :, cols(t)])

    def arrive(chunk):
        own_copy(chunk).wait()
        for turn in range(1, nodes):
            block_copy(chunk, turn).wait_recv()

        @pl.when(has_high)
        def _():
            side_copy(chunk, True).start()

        @pl.when(has_low)
        def _():
            side_copy(chunk, False).start()

    lower3 = lax.broadcasted_iota(jnp.int32, (ROWS // 8, 8, LANE), 2) < NZ

    def apply(chunk):
        @pl.when(has_high)
        def _():
            side_copy(chunk, False).wait_recv()

        @pl.when(has_low)
        def _():
            side_copy(chunk, True).wait_recv()

        rows = pl.ds(chunk * ROWS, ROWS)

        def one(node, carry):
            def wide(value):
                return value.astype(jnp.float32).reshape(ROWS // 8, 8, LANE)

            def load(plane, tile):
                return wide(held[node, plane, rows, cols(tile)])

            sides = [load(plane, tiles) for plane in range(2)]
            now = [load(plane, 0) for plane in range(2)]
            turned = [pltpu.roll(v, NZ, 2) for v in now]
            last = list(sides)
            for t in range(tiles):
                if t + 1 < tiles:
                    later = [load(plane, t + 1) for plane in range(2)]
                    coming = [pltpu.roll(v, NZ, 2) for v in later]
                else:
                    later, coming = (None, list(sides))
                mid = coef[9, :, cols(t)] * (now[0] - now[1])
                beside = [wide(side[p, node, rows, cols(t)]) for p in range(2)]
                for plane in range(2):
                    v = now[plane]
                    up = jnp.where(lower3, turned[plane], coming[plane])
                    down = jnp.where(lower3, last[plane], turned[plane])
                    flux = coef[4 * plane, :, cols(t)] * (v - pltpu.roll(v, LANE - 1, 2))
                    total = flux - pltpu.roll(flux, 1, 2)
                    total = total + coef[4 * plane + 3, :, cols(t)] * v
                    total = total + coef[4 * plane + 1, :, cols(t)] * (v - up)
                    total = total + coef[4 * plane + 2, :, cols(t)] * (v - down)
                    total = total + coef[8 + 2 * plane, :, cols(t)] * (v - beside[plane])
                    total = total - mid if plane else total + mid
                    image[node, plane, rows, cols(t)] = total.reshape(ROWS, LANE).astype(
                        jnp.bfloat16
                    )
                last, turned, now = (turned, coming, later)
            return carry

        lax.fori_loop(0, nodes, one, 0)

    arrive(0)

    def step(chunk, carry):
        arrive(chunk)
        apply(chunk - 1)
        return carry

    lax.fori_loop(1, chunks, step, 0)
    apply(chunks - 1)

    order = nodes * snap_rows
    core = lax.rem(at, 2)
    partner = at + 1 - 2 * core
    layer = at // 2

    def product(pair):
        tile = jnp.zeros((order, 2 * snap_rows), jnp.float32)
        for plane in range(2):
            left = held[:, plane, :, :length].reshape(order, length)
            right = image[pl.ds(2 * pair, 2), plane].reshape(2 * snap_rows, length)
            tile = tile + lax.dot_general(
                left, right, (((1,), (1,)), ((), ())), preferred_element_type=jnp.float32
            )
        for index in range(2):
            part = tile[:, index * snap_rows : (index + 1) * snap_rows]
            gram[2 * pair + index] = part.reshape(gram.shape[1:])

    def first_copy(block):
        return pltpu.make_async_remote_copy(
            src_ref=gram.at[block, :, 1 - core],
            dst_ref=first.at[block],
            send_sem=send1.at[block],
            recv_sem=recv1.at[block],
            device_id={"space": partner},
            device_id_type=MESH,
        )

    share = gram.shape[3]
    early = share * 5 // 8 // 8 * 8
    one, two = (pl.ds(0, early), pl.ds(early, share - early))

    def second_copy(turn):
        block = lax.rem(me + turn, nodes)
        return pltpu.make_async_remote_copy(
            src_ref=first.at[block, :, one],
            dst_ref=second.at[turn - 1],
            send_sem=send2.at[turn - 1],
            recv_sem=recv2.at[turn - 1],
            device_id={"node": block},
            device_id_type=MESH,
        )

    def third_copy(turn):
        return pltpu.make_async_remote_copy(
            src_ref=first.at[me, lax.rem(layer + turn, layers), one],
            dst_ref=third.at[turn - 1],
            send_sem=send3.at[turn - 1],
            recv_sem=recv3.at[turn - 1],
            device_id={"space": lax.rem(at + 2 * turn, spaces)},
            device_id_type=MESH,
        )

    def late_copy(turn):
        return pltpu.make_async_remote_copy(
            src_ref=first.at[:, lax.rem(layer + turn, layers), two],
            dst_ref=late.at[turn - 1],
            send_sem=send4.at[turn - 1],
            recv_sem=recv4.at[turn - 1],
            device_id={"space": lax.rem(at + 2 * turn, spaces)},
            device_id_type=MESH,
        )

    def cross_copy(turn):
        block = lax.rem(me + turn, nodes)
        return pltpu.make_async_remote_copy(
            src_ref=first.at[block, layer, two],
            dst_ref=cross.at[turn - 1],
            send_sem=send5.at[turn - 1],
            recv_sem=recv5.at[turn - 1],
            device_id={"node": block},
            device_id_type=MESH,
        )

    if summed:
        def joined(block):
            first_copy(block).wait_recv()
            first[block] = first[block] + gram[block, :, core]

        away = nodes // 2 - 1 - me // 2
        for index in range(nodes // 2):
            pair = lax.rem(away + index, nodes // 2)
            product(pair)
            for place in range(2):
                first_copy(2 * pair + place).start()
            if index == 0:
                ahead = pair
        for place in range(2):
            block = 2 * ahead + place
            joined(block)
            second_copy(lax.rem(block - me + nodes, nodes)).start()
        block = me + 1 - 2 * lax.rem(me, 2)
        joined(block)
        second_copy(lax.rem(block - me + nodes, nodes)).start()
        joined(me)
        for turn in range(1, layers):
            late_copy(turn).start()
        for turn in range(1, nodes):
            second_copy(turn).wait_recv()
        total = first[me, :, one]
        for turn in range(1, nodes):
            total = total + second[turn - 1]
        first[me, :, one] = total
        for turn in range(1, layers):
            third_copy(turn).start()
        for turn in range(1, layers):
            late_copy(turn).wait_recv()
        total = first[:, layer, two]
        for turn in range(1, layers):
            total = total + late[turn - 1]
        first[:, layer, two] = total
        for turn in range(1, nodes):
            cross_copy(turn).start()
        own = first[me, layer, one]
        for turn in range(1, layers):
            third_copy(turn).wait_recv()
            own = own + third[turn - 1]
        out_ref[one] = own * scale
        own = first[me, layer, two]
        for turn in range(1, nodes):
            cross_copy(turn).wait_recv()
            own = own + cross[turn - 1]
        out_ref[two] = own * scale
        for turn in range(1, nodes):
            cross_copy(turn).wait_send()
        for turn in range(1, layers):
            late_copy(turn).wait_send()
        for turn in range(nodes):
            first_copy(turn).wait_send()
        for turn in range(1, nodes):
            second_copy(turn).wait_send()
        for turn in range(1, layers):
            third_copy(turn).wait_send()
    else:
        for pair in range(nodes // 2):
            product(pair)
        for block in range(nodes):
            out_ref[block * snap_rows : (block + 1) * snap_rows] = gram[block].reshape(
                order, snap_rows
            ).T

    def finish(chunk, carry):
        for turn in range(1, nodes):
            block_copy(chunk, turn).wait_send()

        @pl.when(has_high)
        def _():
            side_copy(chunk, True).wait_send()

        @pl.when(has_low)
        def _():
            side_copy(chunk, False).wait_send()

        return carry

    lax.fori_loop(0, chunks, finish, 0)


def per_device(snapshots, kappa):
    snap_rows, planes, width = snapshots.shape
    nodes, spaces = (lax.axis_size("node"), lax.axis_size("space"))
    length = width // nodes
    chunks = snap_rows // ROWS
    order = nodes * snap_rows
    scale = 1.0 / math.sqrt(planes * spaces * NY * NZ)
    share = order // spaces
    summed = share % 8 == 0 and share * spaces == order and spaces % 2 == 0 and share >= 64
    layers = spaces // 2
    shape = (share, snap_rows) if summed else (order, order)
    early = share * 5 // 8 // 8 * 8 if summed else 8
    blocks = (layers, 2, share) if summed else (1, 1, order)
    result = pl.pallas_call(
        functools.partial(gram_kernel, nodes, spaces, scale),
        out_shape=jax.ShapeDtypeStruct(shape, jnp.float32),
        in_specs=[
            pl.BlockSpec(memory_space=pl.ANY),
            pl.BlockSpec(memory_space=pltpu.VMEM),
        ],
        out_specs=pl.BlockSpec(memory_space=pltpu.VMEM),
        scratch_shapes=[
            pltpu.VMEM((snap_rows, planes, width), jnp.bfloat16),
            pltpu.VMEM((nodes, planes, snap_rows, length + LANE), jnp.bfloat16),
            pltpu.VMEM((nodes, planes, snap_rows, length + LANE), jnp.bfloat16),
            pltpu.VMEM((2, nodes, snap_rows, length), jnp.bfloat16),
            pltpu.VMEM((2, 8, length), jnp.float32),
            pltpu.VMEM((2, 8, length), jnp.float32),
            pltpu.VMEM((11, 8, length), jnp.float32),
            pltpu.VMEM((nodes, planes, snap_rows, length), jnp.bfloat16),
            pltpu.VMEM((nodes,) + blocks + (snap_rows,), jnp.float32),
            pltpu.VMEM((nodes, blocks[0], blocks[2], snap_rows), jnp.float32),
            pltpu.VMEM((nodes - 1, blocks[0], early, snap_rows), jnp.float32),
            pltpu.VMEM((layers - 1, early, snap_rows), jnp.float32),
            pltpu.VMEM((layers - 1, nodes, blocks[2] - early, snap_rows), jnp.float32),
            pltpu.VMEM((nodes - 1, blocks[2] - early, snap_rows), jnp.float32),
            pltpu.SemaphoreType.DMA((chunks,)),
            pltpu.SemaphoreType.DMA((chunks,)),
            pltpu.SemaphoreType.DMA((nodes - 1, chunks)),
            pltpu.SemaphoreType.DMA((nodes - 1, chunks)),
            pltpu.SemaphoreType.DMA((2, chunks)),
            pltpu.SemaphoreType.DMA((2, chunks)),
            pltpu.SemaphoreType.DMA((2,)),
            pltpu.SemaphoreType.DMA((2,)),
            pltpu.SemaphoreType.DMA((nodes,)),
            pltpu.SemaphoreType.DMA((nodes,)),
            pltpu.SemaphoreType.DMA((nodes - 1,)),
            pltpu.SemaphoreType.DMA((nodes - 1,)),
            pltpu.SemaphoreType.DMA((layers - 1,)),
            pltpu.SemaphoreType.DMA((layers - 1,)),
            pltpu.SemaphoreType.DMA((layers - 1,)),
            pltpu.SemaphoreType.DMA((layers - 1,)),
            pltpu.SemaphoreType.DMA((nodes - 1,)),
            pltpu.SemaphoreType.DMA((nodes - 1,)),
        ],
        compiler_params=pltpu.CompilerParams(
            collective_id=0, has_side_effects=True, vmem_limit_bytes=55 * 1024 * 1024
        ),
        name="gram_sums",
    )(
        snapshots,
        kappa,
    )
    if summed:
        return result.T
    mine = lax.psum_scatter(result, "node", scatter_dimension=0, tiled=True)
    return lax.psum_scatter(mine, "space", scatter_dimension=1, tiled=True) * scale


def solution(mesh):
    placed = (P("node", "space", None), P("space", None))
    return jax.shard_map(
        per_device, mesh=mesh, in_specs=placed, out_specs=P("node", "space"), check_vma=False
    )
```

```python
import functools
import math

import jax
import jax.numpy as jnp
from jax import lax
from jax.experimental import pallas as pl
from jax.experimental.pallas import tpu as pltpu
from jax.sharding import PartitionSpec as P

NY = 128
NZ = 64
LANE = 128
ROWS = 16
MESH = pl.DeviceIdType.MESH


def gram_kernel(
    nodes, spaces, scale, snap_ref, kap_ref, out_ref,
    raw, sent, held, side, kown, kside, coef, image, gram, first, second, third, late, cross,
    raw_sem, own_sem, send_sem, recv_sem, hsend, hrecv, ksend, krecv,
    send1, recv1, send2, recv2, send3, recv3, send4, recv4, send5, recv5,
):
    me = lax.axis_index("node")
    at = lax.axis_index("space")
    snap_rows = snap_ref.shape[0]
    length = snap_ref.shape[2] // nodes
    tiles = length // LANE
    chunks = snap_rows // ROWS
    has_low = at > 0
    has_high = at < spaces - 1
    summed = out_ref.shape[0] != nodes * snap_rows
    layers = spaces // 2 if summed else 1

    def raw_copy(chunk):
        rows = pl.ds(chunk * ROWS, ROWS)
        return pltpu.make_async_copy(snap_ref.at[rows], raw.at[rows], raw_sem.at[chunk])

    for chunk in range(chunks):
        raw_copy(chunk).start()

    low_rows = lax.broadcasted_iota(jnp.int32, (ROWS, LANE), 1) < NZ

    def spread(chunk):
        rows = pl.ds(pl.multiple_of(chunk * ROWS, ROWS), ROWS)
        raw_copy(chunk).wait()
        for plane in range(2):

            def turned_tile(first):
                value = raw[rows, plane, first : first + LANE].astype(jnp.float32)
                return pltpu.roll(value, NZ, 1)

            for dest in range(nodes):
                low, high = (dest * length, (dest + 1) * length)
                sent[dest, plane, rows, :length] = raw[rows, plane, low:high]
                before = after = jnp.zeros((ROWS, LANE), jnp.float32)
                if dest:
                    before = turned_tile(low - LANE)
                if dest < nodes - 1:
                    after = turned_tile(high)
                sent[dest, plane, rows, length:] = jnp.where(low_rows, before, after).astype(
                    jnp.bfloat16
                )

    spread(0)
    for plane in range(2):
        values = kap_ref[plane : plane + 1, pl.ds(pl.multiple_of(me * length, LANE), length)]
        kown[plane] = jnp.broadcast_to(values.astype(jnp.float32), (8, length))
    barrier = pltpu.get_barrier_semaphore()
    for turn in range(1, nodes):
        pl.semaphore_signal(
            barrier, inc=1, device_id={"node": lax.rem(me + turn, nodes)}, device_id_type=MESH
        )
    for turn in range(1, layers):
        pl.semaphore_signal(
            barrier,
            inc=1,
            device_id={"space": lax.rem(at + 2 * turn, spaces)},
            device_id_type=MESH,
        )

    @pl.when(has_low)
    def _():
        pl.semaphore_signal(barrier, inc=1, device_id={"space": at - 1}, device_id_type=MESH)

    @pl.when(has_high)
    def _():
        pl.semaphore_signal(barrier, inc=1, device_id={"space": at + 1}, device_id_type=MESH)

    @pl.when(jnp.logical_not(has_low))
    def _():
        side[0] = jnp.zeros(side.shape[1:], side.dtype)
        kside[0] = jnp.zeros(kside.shape[1:], kside.dtype)

    @pl.when(jnp.logical_not(has_high))
    def _():
        side[1] = jnp.zeros(side.shape[1:], side.dtype)
        kside[1] = jnp.zeros(kside.shape[1:], kside.dtype)

    both = jnp.logical_and(has_low, has_high)

    @pl.when(both)
    def _():
        pl.semaphore_wait(barrier, nodes + layers)

    @pl.when(jnp.logical_not(both))
    def _():
        pl.semaphore_wait(barrier, nodes + layers - 1)

    def own_copy(chunk):
        rows = pl.ds(chunk * ROWS, ROWS)
        return pltpu.make_async_copy(
            sent.at[me, :, rows],
            held.at[me, :, rows],
            own_sem.at[chunk],
        )

    def block_copy(chunk, turn):
        rows = pl.ds(chunk * ROWS, ROWS)
        peer = lax.rem(me + turn, nodes)
        return pltpu.make_async_remote_copy(
            src_ref=sent.at[peer, :, rows],
            dst_ref=held.at[me, :, rows],
            send_sem=send_sem.at[turn - 1, chunk],
            recv_sem=recv_sem.at[turn - 1, chunk],
            device_id={"node": peer},
            device_id_type=MESH,
        )

    def side_copy(chunk, high):
        rows = pl.ds(chunk * ROWS, ROWS)
        return pltpu.make_async_remote_copy(
            src_ref=held.at[:, 1 if high else 0, rows, pl.ds(0, length)],
            dst_ref=side.at[0 if high else 1, :, rows],
            send_sem=hsend.at[0 if high else 1, chunk],
            recv_sem=hrecv.at[0 if high else 1, chunk],
            device_id={"space": at + 1 if high else at - 1},
            device_id_type=MESH,
        )

    def kappa_copy(high):
        return pltpu.make_async_remote_copy(
            src_ref=kown.at[1 if high else 0],
            dst_ref=kside.at[0 if high else 1],
            send_sem=ksend.at[0 if high else 1],
            recv_sem=krecv.at[0 if high else 1],
            device_id={"space": at + 1 if high else at - 1},
            device_id_type=MESH,
        )

    @pl.when(has_high)
    def _():
        kappa_copy(True).start()

    @pl.when(has_low)
    def _():
        kappa_copy(False).start()

    def begin(chunk, carry):
        own_copy(chunk).start()
        for turn in range(1, nodes):
            block_copy(chunk, turn).start()
        return carry

    begin(0, 0)

    def follow(chunk, carry):
        spread(chunk)
        return begin(chunk, carry)

    lax.fori_loop(1, chunks, follow, 0)

    @pl.when(has_high)
    def _():
        kappa_copy(True).wait_send()
        kappa_copy(False).wait_recv()

    @pl.when(has_low)
    def _():
        kappa_copy(False).wait_send()
        kappa_copy(True).wait_recv()

    lane = lax.broadcasted_iota(jnp.int32, (8, LANE), 1)
    lower = lane < NZ
    zpos = lane % NZ
    inner = jnp.where(zpos == NZ - 1, 0.0, 0.5).astype(jnp.float32)
    rim = jnp.where(zpos == 0, 0.5, jnp.where(zpos == NZ - 1, 0.5, 0.0)).astype(jnp.float32)

    def cols(tile):
        return pl.ds(tile * LANE, LANE)

    low_at = pl.ds(pl.multiple_of(jnp.maximum(me * tiles - 1, 0) * LANE, LANE), LANE)
    high_at = pl.ds(
        pl.multiple_of(jnp.minimum((me + 1) * tiles, nodes * tiles - 1) * LANE, LANE), LANE
    )
    for plane in range(2):

        def beyond(place):
            value = kap_ref[plane : plane + 1, place].astype(jnp.float32)
            return pltpu.roll(jnp.broadcast_to(value, (8, LANE)), NZ, 1)

        kap = [kown[plane, :, cols(t)] for t in range(tiles)]
        turned = [pltpu.roll(k, NZ, 1) for k in kap]
        before = beyond(low_at)
        after = beyond(high_at)
        before = before * jnp.where(me > 0, 1.0, 0.0)
        after = after * jnp.where(me < nodes - 1, 1.0, 0.0)
        for t in range(tiles):
            k = kap[t]
            up = jnp.where(lower, turned[t], turned[t + 1] if t + 1 < tiles else after)
            down = jnp.where(lower, turned[t - 1] if t else before, turned[t])
            coef[4 * plane, :, cols(t)] = inner * (k + pltpu.roll(k, LANE - 1, 1))
            coef[4 * plane + 1, :, cols(t)] = 0.5 * (k + up)
            coef[4 * plane + 2, :, cols(t)] = 0.5 * (k + down)
            coef[4 * plane + 3, :, cols(t)] = rim * k
    for t in range(tiles):
        low, high = (kown[0, :, cols(t)], kown[1, :, cols(t)])
        coef[8, :, cols(t)] = 0.5 * (low + kside[0, :, cols(t)])
        coef[9, :, cols(t)] = 0.5 * (low + high)
        coef[10, :, cols(t)] = 0.5 * (high + kside[1, :, cols(t)])

    def arrive(chunk):
        own_copy(chunk).wait()
        for turn in range(1, nodes):
            block_copy(chunk, turn).wait_recv()

        @pl.when(has_high)
        def _():
            side_copy(chunk, True).start()

        @pl.when(has_low)
        def _():
            side_copy(chunk, False).start()

    lower3 = lax.broadcasted_iota(jnp.int32, (ROWS // 4, 8, LANE), 2) < NZ

    def apply(chunk):
        @pl.when(has_high)
        def _():
            side_copy(chunk, False).wait_recv()

        @pl.when(has_low)
        def _():
            side_copy(chunk, True).wait_recv()

        rows = pl.ds(chunk * ROWS, ROWS)

        def one(index, carry):
            node = pl.ds(2 * index, 2)
            ready = []

            def wide(value):
                return value.astype(jnp.float32).reshape(ROWS // 4, 8, LANE)

            def load(plane, tile):
                return wide(held[node, plane, rows, cols(tile)])

            sides = [load(plane, tiles) for plane in range(2)]
            now = [load(plane, 0) for plane in range(2)]
            turned = [pltpu.roll(v, NZ, 2) for v in now]
            last = list(sides)
            for t in range(tiles):
                if t + 1 < tiles:
                    later = [load(plane, t + 1) for plane in range(2)]
                    coming = [pltpu.roll(v, NZ, 2) for v in later]
                else:
                    later, coming = (None, list(sides))
                mid = coef[9, :, cols(t)] * (now[0] - now[1])
                beside = [wide(side[p, node, rows, cols(t)]) for p in range(2)]
                for plane in range(2):
                    v = now[plane]
                    up = jnp.where(lower3, turned[plane], coming[plane])
                    down = jnp.where(lower3, last[plane], turned[plane])
                    flux = coef[4 * plane, :, cols(t)] * (v - pltpu.roll(v, LANE - 1, 2))
                    total = flux - pltpu.roll(flux, 1, 2)
                    total = total + coef[4 * plane + 3, :, cols(t)] * v
                    total = total + coef[4 * plane + 1, :, cols(t)] * (v - up)
                    total = total + coef[4 * plane + 2, :, cols(t)] * (v - down)
                    total = total + coef[8 + 2 * plane, :, cols(t)] * (v - beside[plane])
                    total = total - mid if plane else total + mid
                    ready.append(total.reshape(2, ROWS, LANE).astype(jnp.bfloat16))
                if t:
                    for plane in range(2):
                        image[node, plane, rows, cols(t - 1)] = ready.pop(0)
                last, turned, now = (turned, coming, later)
            for plane in range(2):
                image[node, plane, rows, cols(tiles - 1)] = ready.pop(0)
            return carry

        lax.fori_loop(0, nodes // 2, one, 0)

    arrive(0)

    def step(chunk, carry):
        arrive(chunk)
        apply(chunk - 1)
        return carry

    lax.fori_loop(1, chunks, step, 0)
    apply(chunks - 1)

    order = nodes * snap_rows
    core = lax.rem(at, 2)
    partner = at + 1 - 2 * core
    layer = at // 2

    def product(pair):
        tile = jnp.zeros((order, 2 * snap_rows), jnp.float32)
        for plane in range(2):
            left = held[:, plane, :, :length].reshape(order, length)
            right = image[pl.ds(2 * pair, 2), plane].reshape(2 * snap_rows, length)
            tile = tile + lax.dot_general(
                left, right, (((1,), (1,)), ((), ())), preferred_element_type=jnp.float32
            )
        for index in range(2):
            part = tile[:, index * snap_rows : (index + 1) * snap_rows]
            gram[2 * pair + index] = part.reshape(gram.shape[1:])

    def first_copy(block):
        return pltpu.make_async_remote_copy(
            src_ref=gram.at[block, :, 1 - core],
            dst_ref=first.at[block],
            send_sem=send1.at[block],
            recv_sem=recv1.at[block],
            device_id={"space": partner},
            device_id_type=MESH,
        )

    share = gram.shape[3]
    early = share * 5 // 8 // 8 * 8
    one, two = (pl.ds(0, early), pl.ds(early, share - early))

    def second_copy(turn):
        block = lax.rem(me + turn, nodes)
        return pltpu.make_async_remote_copy(
            src_ref=first.at[block, :, one],
            dst_ref=second.at[turn - 1],
            send_sem=send2.at[turn - 1],
            recv_sem=recv2.at[turn - 1],
            device_id={"node": block},
            device_id_type=MESH,
        )

    def third_copy(turn):
        return pltpu.make_async_remote_copy(
            src_ref=first.at[me, lax.rem(layer + turn, layers), one],
            dst_ref=third.at[turn - 1],
            send_sem=send3.at[turn - 1],
            recv_sem=recv3.at[turn - 1],
            device_id={"space": lax.rem(at + 2 * turn, spaces)},
            device_id_type=MESH,
        )

    def late_copy(turn):
        return pltpu.make_async_remote_copy(
            src_ref=first.at[:, lax.rem(layer + turn, layers), two],
            dst_ref=late.at[turn - 1],
            send_sem=send4.at[turn - 1],
            recv_sem=recv4.at[turn - 1],
            device_id={"space": lax.rem(at + 2 * turn, spaces)},
            device_id_type=MESH,
        )

    def cross_copy(turn):
        block = lax.rem(me + turn, nodes)
        return pltpu.make_async_remote_copy(
            src_ref=first.at[block, layer, two],
            dst_ref=cross.at[turn - 1],
            send_sem=send5.at[turn - 1],
            recv_sem=recv5.at[turn - 1],
            device_id={"node": block},
            device_id_type=MESH,
        )

    if summed:
        def joined(block):
            first_copy(block).wait_recv()
            first[block] = first[block] + gram[block, :, core]

        away = nodes // 2 - 1 - me // 2
        for index in range(nodes // 2):
            pair = lax.rem(away + index, nodes // 2)
            product(pair)
            for place in range(2):
                first_copy(2 * pair + place).start()
            if index == 0:
                ahead = pair
        for place in range(2):
            block = 2 * ahead + place
            joined(block)
            second_copy(lax.rem(block - me + nodes, nodes)).start()
        block = me + 1 - 2 * lax.rem(me, 2)
        joined(block)
        second_copy(lax.rem(block - me + nodes, nodes)).start()
        joined(me)
        for turn in range(1, layers):
            late_copy(turn).start()
        for turn in range(1, nodes):
            second_copy(turn).wait_recv()
        total = first[me, :, one]
        for turn in range(1, nodes):
            total = total + second[turn - 1]
        first[me, :, one] = total
        for turn in range(1, layers):
            third_copy(turn).start()
        for turn in range(1, layers):
            late_copy(turn).wait_recv()
        total = first[:, layer, two]
        for turn in range(1, layers):
            total = total + late[turn - 1]
        first[:, layer, two] = total
        for turn in range(1, nodes):
            cross_copy(turn).start()
        own = first[me, layer, one]
        for turn in range(1, layers):
            third_copy(turn).wait_recv()
            own = own + third[turn - 1]
        out_ref[one] = own * scale
        own = first[me, layer, two]
        for turn in range(1, nodes):
            cross_copy(turn).wait_recv()
            own = own + cross[turn - 1]
        out_ref[two] = own * scale
        for turn in range(1, nodes):
            cross_copy(turn).wait_send()
        for turn in range(1, layers):
            late_copy(turn).wait_send()
        for turn in range(nodes):
            first_copy(turn).wait_send()
        for turn in range(1, nodes):
            second_copy(turn).wait_send()
        for turn in range(1, layers):
            third_copy(turn).wait_send()
    else:
        for pair in range(nodes // 2):
            product(pair)
        for block in range(nodes):
            out_ref[block * snap_rows : (block + 1) * snap_rows] = gram[block].reshape(
                order, snap_rows
            ).T

    def finish(chunk, carry):
        for turn in range(1, nodes):
            block_copy(chunk, turn).wait_send()

        @pl.when(has_high)
        def _():
            side_copy(chunk, True).wait_send()

        @pl.when(has_low)
        def _():
            side_copy(chunk, False).wait_send()

        return carry

    lax.fori_loop(0, chunks, finish, 0)


def per_device(snapshots, kappa):
    snap_rows, planes, width = snapshots.shape
    nodes, spaces = (lax.axis_size("node"), lax.axis_size("space"))
    length = width // nodes
    chunks = snap_rows // ROWS
    order = nodes * snap_rows
    scale = 1.0 / math.sqrt(planes * spaces * NY * NZ)
    share = order // spaces
    summed = share % 8 == 0 and share * spaces == order and spaces % 2 == 0 and share >= 64
    layers = spaces // 2
    shape = (share, snap_rows) if summed else (order, order)
    early = share * 5 // 8 // 8 * 8 if summed else 8
    blocks = (layers, 2, share) if summed else (1, 1, order)
    result = pl.pallas_call(
        functools.partial(gram_kernel, nodes, spaces, scale),
        out_shape=jax.ShapeDtypeStruct(shape, jnp.float32),
        in_specs=[
            pl.BlockSpec(memory_space=pl.ANY),
            pl.BlockSpec(memory_space=pltpu.VMEM),
        ],
        out_specs=pl.BlockSpec(memory_space=pltpu.VMEM),
        scratch_shapes=[
            pltpu.VMEM((snap_rows, planes, width), jnp.bfloat16),
            pltpu.VMEM((nodes, planes, snap_rows, length + LANE), jnp.bfloat16),
            pltpu.VMEM((nodes, planes, snap_rows, length + LANE), jnp.bfloat16),
            pltpu.VMEM((2, nodes, snap_rows, length), jnp.bfloat16),
            pltpu.VMEM((2, 8, length), jnp.float32),
            pltpu.VMEM((2, 8, length), jnp.float32),
            pltpu.VMEM((11, 8, length), jnp.float32),
            pltpu.VMEM((nodes, planes, snap_rows, length), jnp.bfloat16),
            pltpu.VMEM((nodes,) + blocks + (snap_rows,), jnp.float32),
            pltpu.VMEM((nodes, blocks[0], blocks[2], snap_rows), jnp.float32),
            pltpu.VMEM((nodes - 1, blocks[0], early, snap_rows), jnp.float32),
            pltpu.VMEM((layers - 1, early, snap_rows), jnp.float32),
            pltpu.VMEM((layers - 1, nodes, blocks[2] - early, snap_rows), jnp.float32),
            pltpu.VMEM((nodes - 1, blocks[2] - early, snap_rows), jnp.float32),
            pltpu.SemaphoreType.DMA((chunks,)),
            pltpu.SemaphoreType.DMA((chunks,)),
            pltpu.SemaphoreType.DMA((nodes - 1, chunks)),
            pltpu.SemaphoreType.DMA((nodes - 1, chunks)),
            pltpu.SemaphoreType.DMA((2, chunks)),
            pltpu.SemaphoreType.DMA((2, chunks)),
            pltpu.SemaphoreType.DMA((2,)),
            pltpu.SemaphoreType.DMA((2,)),
            pltpu.SemaphoreType.DMA((nodes,)),
            pltpu.SemaphoreType.DMA((nodes,)),
            pltpu.SemaphoreType.DMA((nodes - 1,)),
            pltpu.SemaphoreType.DMA((nodes - 1,)),
            pltpu.SemaphoreType.DMA((layers - 1,)),
            pltpu.SemaphoreType.DMA((layers - 1,)),
            pltpu.SemaphoreType.DMA((layers - 1,)),
            pltpu.SemaphoreType.DMA((layers - 1,)),
            pltpu.SemaphoreType.DMA((nodes - 1,)),
            pltpu.SemaphoreType.DMA((nodes - 1,)),
        ],
        compiler_params=pltpu.CompilerParams(
            collective_id=0, has_side_effects=True, vmem_limit_bytes=52 * 1024 * 1024
        ),
        name="gram_sums",
    )(
        snapshots,
        kappa,
    )
    if summed:
        return result.T
    mine = lax.psum_scatter(result, "node", scatter_dimension=0, tiled=True)
    return lax.psum_scatter(mine, "space", scatter_dimension=1, tiled=True) * scale


def solution(mesh):
    placed = (P("node", "space", None), P("space", None))
    return jax.shard_map(
        per_device, mesh=mesh, in_specs=placed, out_specs=P("node", "space"), check_vma=False
    )
```

```python
import functools
import math

import jax
import jax.numpy as jnp
from jax import lax
from jax.experimental import pallas as pl
from jax.experimental.pallas import tpu as pltpu
from jax.sharding import PartitionSpec as P

NY = 128
NZ = 64
LANE = 128
ROWS = 16
MESH = pl.DeviceIdType.MESH


def gram_kernel(
    nodes, spaces, scale, snap_ref, kap_ref, out_ref,
    raw, sent, held, side, kown, kside, coef, image, gram, first, second, third, late, cross,
    raw_sem, own_sem, send_sem, recv_sem, hsend, hrecv, ksend, krecv,
    send1, recv1, send2, recv2, send3, recv3, send4, recv4, send5, recv5,
):
    me = lax.axis_index("node")
    at = lax.axis_index("space")
    snap_rows = snap_ref.shape[0]
    length = snap_ref.shape[2] // nodes
    tiles = length // LANE
    chunks = snap_rows // ROWS
    has_low = at > 0
    has_high = at < spaces - 1
    summed = out_ref.shape[0] != nodes * snap_rows
    layers = spaces // 2 if summed else 1

    def raw_copy(chunk):
        rows = pl.ds(chunk * ROWS, ROWS)
        return pltpu.make_async_copy(snap_ref.at[rows], raw.at[rows], raw_sem.at[chunk])

    raw_copy(0).start()

    low_rows = lax.broadcasted_iota(jnp.int32, (ROWS, LANE), 1) < NZ

    def spread(chunk):
        rows = pl.ds(pl.multiple_of(chunk * ROWS, ROWS), ROWS)
        raw_copy(chunk).wait()
        for plane in range(2):

            def turned_tile(first):
                value = raw[rows, plane, first : first + LANE].astype(jnp.float32)
                return pltpu.roll(value, NZ, 1)

            for dest in range(nodes):
                low, high = (dest * length, (dest + 1) * length)
                sent[dest, plane, rows, :length] = raw[rows, plane, low:high]
                before = after = jnp.zeros((ROWS, LANE), jnp.float32)
                if dest:
                    before = turned_tile(low - LANE)
                if dest < nodes - 1:
                    after = turned_tile(high)
                sent[dest, plane, rows, length:] = jnp.where(low_rows, before, after).astype(
                    jnp.bfloat16
                )

    spread(0)
    for chunk in range(1, chunks):
        raw_copy(chunk).start()
    for plane in range(2):
        values = kap_ref[plane : plane + 1, pl.ds(pl.multiple_of(me * length, LANE), length)]
        kown[plane] = jnp.broadcast_to(values.astype(jnp.float32), (8, length))
    barrier = pltpu.get_barrier_semaphore()
    for turn in range(1, nodes):
        pl.semaphore_signal(
            barrier, inc=1, device_id={"node": lax.rem(me + turn, nodes)}, device_id_type=MESH
        )
    for turn in range(1, layers):
        pl.semaphore_signal(
            barrier,
            inc=1,
            device_id={"space": lax.rem(at + 2 * turn, spaces)},
            device_id_type=MESH,
        )

    @pl.when(has_low)
    def _():
        pl.semaphore_signal(barrier, inc=1, device_id={"space": at - 1}, device_id_type=MESH)

    @pl.when(has_high)
    def _():
        pl.semaphore_signal(barrier, inc=1, device_id={"space": at + 1}, device_id_type=MESH)

    @pl.when(jnp.logical_not(has_low))
    def _():
        side[0] = jnp.zeros(side.shape[1:], side.dtype)
        kside[0] = jnp.zeros(kside.shape[1:], kside.dtype)

    @pl.when(jnp.logical_not(has_high))
    def _():
        side[1] = jnp.zeros(side.shape[1:], side.dtype)
        kside[1] = jnp.zeros(kside.shape[1:], kside.dtype)

    both = jnp.logical_and(has_low, has_high)

    @pl.when(both)
    def _():
        pl.semaphore_wait(barrier, nodes + layers)

    @pl.when(jnp.logical_not(both))
    def _():
        pl.semaphore_wait(barrier, nodes + layers - 1)

    def own_copy(chunk):
        rows = pl.ds(chunk * ROWS, ROWS)
        return pltpu.make_async_copy(
            sent.at[me, :, rows],
            held.at[me, :, rows],
            own_sem.at[chunk],
        )

    def block_copy(chunk, turn):
        rows = pl.ds(chunk * ROWS, ROWS)
        peer = lax.rem(me + turn, nodes)
        return pltpu.make_async_remote_copy(
            src_ref=sent.at[peer, :, rows],
            dst_ref=held.at[me, :, rows],
            send_sem=send_sem.at[turn - 1, chunk],
            recv_sem=recv_sem.at[turn - 1, chunk],
            device_id={"node": peer},
            device_id_type=MESH,
        )

    def side_copy(chunk, high):
        rows = pl.ds(chunk * ROWS, ROWS)
        return pltpu.make_async_remote_copy(
            src_ref=held.at[:, 1 if high else 0, rows, pl.ds(0, length)],
            dst_ref=side.at[0 if high else 1, :, rows],
            send_sem=hsend.at[0 if high else 1, chunk],
            recv_sem=hrecv.at[0 if high else 1, chunk],
            device_id={"space": at + 1 if high else at - 1},
            device_id_type=MESH,
        )

    def kappa_copy(high):
        return pltpu.make_async_remote_copy(
            src_ref=kown.at[1 if high else 0],
            dst_ref=kside.at[0 if high else 1],
            send_sem=ksend.at[0 if high else 1],
            recv_sem=krecv.at[0 if high else 1],
            device_id={"space": at + 1 if high else at - 1},
            device_id_type=MESH,
        )

    @pl.when(has_high)
    def _():
        kappa_copy(True).start()

    @pl.when(has_low)
    def _():
        kappa_copy(False).start()

    def begin(chunk, carry):
        own_copy(chunk).start()
        for turn in range(1, nodes):
            block_copy(chunk, turn).start()
        return carry

    begin(0, 0)

    def follow(chunk, carry):
        spread(chunk)
        return begin(chunk, carry)

    lax.fori_loop(1, chunks, follow, 0)

    @pl.when(has_high)
    def _():
        kappa_copy(True).wait_send()
        kappa_copy(False).wait_recv()

    @pl.when(has_low)
    def _():
        kappa_copy(False).wait_send()
        kappa_copy(True).wait_recv()

    lane = lax.broadcasted_iota(jnp.int32, (8, LANE), 1)
    lower = lane < NZ
    zpos = lane % NZ
    inner = jnp.where(zpos == NZ - 1, 0.0, 0.5).astype(jnp.float32)
    rim = jnp.where(zpos == 0, 0.5, jnp.where(zpos == NZ - 1, 0.5, 0.0)).astype(jnp.float32)

    def cols(tile):
        return pl.ds(tile * LANE, LANE)

    low_at = pl.ds(pl.multiple_of(jnp.maximum(me * tiles - 1, 0) * LANE, LANE), LANE)
    high_at = pl.ds(
        pl.multiple_of(jnp.minimum((me + 1) * tiles, nodes * tiles - 1) * LANE, LANE), LANE
    )
    for plane in range(2):

        def beyond(place):
            value = kap_ref[plane : plane + 1, place].astype(jnp.float32)
            return pltpu.roll(jnp.broadcast_to(value, (8, LANE)), NZ, 1)

        kap = [kown[plane, :, cols(t)] for t in range(tiles)]
        turned = [pltpu.roll(k, NZ, 1) for k in kap]
        before = beyond(low_at)
        after = beyond(high_at)
        before = before * jnp.where(me > 0, 1.0, 0.0)
        after = after * jnp.where(me < nodes - 1, 1.0, 0.0)
        for t in range(tiles):
            k = kap[t]
            up = jnp.where(lower, turned[t], turned[t + 1] if t + 1 < tiles else after)
            down = jnp.where(lower, turned[t - 1] if t else before, turned[t])
            coef[4 * plane, :, cols(t)] = inner * (k + pltpu.roll(k, LANE - 1, 1))
            coef[4 * plane + 1, :, cols(t)] = 0.5 * (k + up)
            coef[4 * plane + 2, :, cols(t)] = 0.5 * (k + down)
            coef[4 * plane + 3, :, cols(t)] = rim * k
    for t in range(tiles):
        low, high = (kown[0, :, cols(t)], kown[1, :, cols(t)])
        coef[8, :, cols(t)] = 0.5 * (low + kside[0, :, cols(t)])
        coef[9, :, cols(t)] = 0.5 * (low + high)
        coef[10, :, cols(t)] = 0.5 * (high + kside[1, :, cols(t)])

    def arrive(chunk):
        own_copy(chunk).wait()
        for turn in range(1, nodes):
            block_copy(chunk, turn).wait_recv()

        @pl.when(has_high)
        def _():
            side_copy(chunk, True).start()

        @pl.when(has_low)
        def _():
            side_copy(chunk, False).start()

    lower3 = lax.broadcasted_iota(jnp.int32, (ROWS // 8, 8, LANE), 2) < NZ

    def apply(chunk):
        @pl.when(has_high)
        def _():
            side_copy(chunk, False).wait_recv()

        @pl.when(has_low)
        def _():
            side_copy(chunk, True).wait_recv()

        rows = pl.ds(chunk * ROWS, ROWS)

        def one(node, carry):
            def wide(value):
                return value.astype(jnp.float32).reshape(ROWS // 8, 8, LANE)

            def load(plane, tile):
                return wide(held[node, plane, rows, cols(tile)])

            sides = [load(plane, tiles) for plane in range(2)]
            now = [load(plane, 0) for plane in range(2)]
            turned = [pltpu.roll(v, NZ, 2) for v in now]
            last = list(sides)
            for t in range(tiles):
                if t + 1 < tiles:
                    later = [load(plane, t + 1) for plane in range(2)]
                    coming = [pltpu.roll(v, NZ, 2) for v in later]
                else:
                    later, coming = (None, list(sides))
                mid = coef[9, :, cols(t)] * (now[0] - now[1])
                beside = [wide(side[p, node, rows, cols(t)]) for p in range(2)]
                for plane in range(2):
                    v = now[plane]
                    up = jnp.where(lower3, turned[plane], coming[plane])
                    down = jnp.where(lower3, last[plane], turned[plane])
                    flux = coef[4 * plane, :, cols(t)] * (v - pltpu.roll(v, LANE - 1, 2))
                    total = flux - pltpu.roll(flux, 1, 2)
                    total = total + coef[4 * plane + 3, :, cols(t)] * v
                    total = total + coef[4 * plane + 1, :, cols(t)] * (v - up)
                    total = total + coef[4 * plane + 2, :, cols(t)] * (v - down)
                    total = total + coef[8 + 2 * plane, :, cols(t)] * (v - beside[plane])
                    total = total - mid if plane else total + mid
                    image[node, plane, rows, cols(t)] = total.reshape(ROWS, LANE).astype(
                        jnp.bfloat16
                    )
                last, turned, now = (turned, coming, later)
            return carry

        lax.fori_loop(0, nodes, one, 0)

    arrive(0)

    def step(chunk, carry):
        arrive(chunk)
        apply(chunk - 1)
        return carry

    lax.fori_loop(1, chunks, step, 0)
    apply(chunks - 1)

    order = nodes * snap_rows
    core = lax.rem(at, 2)
    partner = at + 1 - 2 * core
    layer = at // 2

    def product(pair):
        tile = jnp.zeros((order, 2 * snap_rows), jnp.float32)
        for plane in range(2):
            left = held[:, plane, :, :length].reshape(order, length)
            right = image[pl.ds(2 * pair, 2), plane].reshape(2 * snap_rows, length)
            tile = tile + lax.dot_general(
                left, right, (((1,), (1,)), ((), ())), preferred_element_type=jnp.float32
            )
        for index in range(2):
            part = tile[:, index * snap_rows : (index + 1) * snap_rows]
            gram[2 * pair + index] = part.reshape(gram.shape[1:])

    def first_copy(block):
        return pltpu.make_async_remote_copy(
            src_ref=gram.at[block, :, 1 - core],
            dst_ref=first.at[block],
            send_sem=send1.at[block],
            recv_sem=recv1.at[block],
            device_id={"space": partner},
            device_id_type=MESH,
        )

    share = gram.shape[3]
    early = share * 5 // 8 // 8 * 8
    one, two = (pl.ds(0, early), pl.ds(early, share - early))

    def second_copy(turn):
        block = lax.rem(me + turn, nodes)
        return pltpu.make_async_remote_copy(
            src_ref=first.at[block, :, one],
            dst_ref=second.at[turn - 1],
            send_sem=send2.at[turn - 1],
            recv_sem=recv2.at[turn - 1],
            device_id={"node": block},
            device_id_type=MESH,
        )

    def third_copy(turn):
        return pltpu.make_async_remote_copy(
            src_ref=first.at[me, lax.rem(layer + turn, layers), one],
            dst_ref=third.at[turn - 1],
            send_sem=send3.at[turn - 1],
            recv_sem=recv3.at[turn - 1],
            device_id={"space": lax.rem(at + 2 * turn, spaces)},
            device_id_type=MESH,
        )

    def late_copy(turn):
        return pltpu.make_async_remote_copy(
            src_ref=first.at[:, lax.rem(layer + turn, layers), two],
            dst_ref=late.at[turn - 1],
            send_sem=send4.at[turn - 1],
            recv_sem=recv4.at[turn - 1],
            device_id={"space": lax.rem(at + 2 * turn, spaces)},
            device_id_type=MESH,
        )

    def cross_copy(turn):
        block = lax.rem(me + turn, nodes)
        return pltpu.make_async_remote_copy(
            src_ref=first.at[block, layer, two],
            dst_ref=cross.at[turn - 1],
            send_sem=send5.at[turn - 1],
            recv_sem=recv5.at[turn - 1],
            device_id={"node": block},
            device_id_type=MESH,
        )

    if summed:
        def joined(block):
            first_copy(block).wait_recv()
            first[block] = first[block] + gram[block, :, core]

        away = nodes // 2 - 1 - me // 2
        for index in range(nodes // 2):
            pair = lax.rem(away + index, nodes // 2)
            product(pair)
            for place in range(2):
                first_copy(2 * pair + place).start()
            if index == 0:
                ahead = pair
        for place in range(2):
            block = 2 * ahead + place
            joined(block)
            second_copy(lax.rem(block - me + nodes, nodes)).start()
        block = me + 1 - 2 * lax.rem(me, 2)
        joined(block)
        second_copy(lax.rem(block - me + nodes, nodes)).start()
        joined(me)
        for turn in range(1, layers):
            late_copy(turn).start()
        for turn in range(1, nodes):
            second_copy(turn).wait_recv()
        total = first[me, :, one]
        for turn in range(1, nodes):
            total = total + second[turn - 1]
        first[me, :, one] = total
        for turn in range(1, layers):
            third_copy(turn).start()
        for turn in range(1, layers):
            late_copy(turn).wait_recv()
        total = first[:, layer, two]
        for turn in range(1, layers):
            total = total + late[turn - 1]
        first[:, layer, two] = total
        for turn in range(1, nodes):
            cross_copy(turn).start()
        own = first[me, layer, one]
        for turn in range(1, layers):
            third_copy(turn).wait_recv()
            own = own + third[turn - 1]
        out_ref[one] = own * scale
        own = first[me, layer, two]
        for turn in range(1, nodes):
            cross_copy(turn).wait_recv()
            own = own + cross[turn - 1]
        out_ref[two] = own * scale
        for turn in range(1, nodes):
            cross_copy(turn).wait_send()
        for turn in range(1, layers):
            late_copy(turn).wait_send()
        for turn in range(nodes):
            first_copy(turn).wait_send()
        for turn in range(1, nodes):
            second_copy(turn).wait_send()
        for turn in range(1, layers):
            third_copy(turn).wait_send()
    else:
        for pair in range(nodes // 2):
            product(pair)
        for block in range(nodes):
            out_ref[block * snap_rows : (block + 1) * snap_rows] = gram[block].reshape(
                order, snap_rows
            ).T

    def finish(chunk, carry):
        for turn in range(1, nodes):
            block_copy(chunk, turn).wait_send()

        @pl.when(has_high)
        def _():
            side_copy(chunk, True).wait_send()

        @pl.when(has_low)
        def _():
            side_copy(chunk, False).wait_send()

        return carry

    lax.fori_loop(0, chunks, finish, 0)


def per_device(snapshots, kappa):
    snap_rows, planes, width = snapshots.shape
    nodes, spaces = (lax.axis_size("node"), lax.axis_size("space"))
    length = width // nodes
    chunks = snap_rows // ROWS
    order = nodes * snap_rows
    scale = 1.0 / math.sqrt(planes * spaces * NY * NZ)
    share = order // spaces
    summed = share % 8 == 0 and share * spaces == order and spaces % 2 == 0 and share >= 64
    layers = spaces // 2
    shape = (share, snap_rows) if summed else (order, order)
    early = share * 5 // 8 // 8 * 8 if summed else 8
    blocks = (layers, 2, share) if summed else (1, 1, order)
    result = pl.pallas_call(
        functools.partial(gram_kernel, nodes, spaces, scale),
        out_shape=jax.ShapeDtypeStruct(shape, jnp.float32),
        in_specs=[
            pl.BlockSpec(memory_space=pl.ANY),
            pl.BlockSpec(memory_space=pltpu.VMEM),
        ],
        out_specs=pl.BlockSpec(memory_space=pltpu.VMEM),
        scratch_shapes=[
            pltpu.VMEM((snap_rows, planes, width), jnp.bfloat16),
            pltpu.VMEM((nodes, planes, snap_rows, length + LANE), jnp.bfloat16),
            pltpu.VMEM((nodes, planes, snap_rows, length + LANE), jnp.bfloat16),
            pltpu.VMEM((2, nodes, snap_rows, length), jnp.bfloat16),
            pltpu.VMEM((2, 8, length), jnp.float32),
            pltpu.VMEM((2, 8, length), jnp.float32),
            pltpu.VMEM((11, 8, length), jnp.float32),
            pltpu.VMEM((nodes, planes, snap_rows, length), jnp.bfloat16),
            pltpu.VMEM((nodes,) + blocks + (snap_rows,), jnp.float32),
            pltpu.VMEM((nodes, blocks[0], blocks[2], snap_rows), jnp.float32),
            pltpu.VMEM((nodes - 1, blocks[0], early, snap_rows), jnp.float32),
            pltpu.VMEM((layers - 1, early, snap_rows), jnp.float32),
            pltpu.VMEM((layers - 1, nodes, blocks[2] - early, snap_rows), jnp.float32),
            pltpu.VMEM((nodes - 1, blocks[2] - early, snap_rows), jnp.float32),
            pltpu.SemaphoreType.DMA((chunks,)),
            pltpu.SemaphoreType.DMA((chunks,)),
            pltpu.SemaphoreType.DMA((nodes - 1, chunks)),
            pltpu.SemaphoreType.DMA((nodes - 1, chunks)),
            pltpu.SemaphoreType.DMA((2, chunks)),
            pltpu.SemaphoreType.DMA((2, chunks)),
            pltpu.SemaphoreType.DMA((2,)),
            pltpu.SemaphoreType.DMA((2,)),
            pltpu.SemaphoreType.DMA((nodes,)),
            pltpu.SemaphoreType.DMA((nodes,)),
            pltpu.SemaphoreType.DMA((nodes - 1,)),
            pltpu.SemaphoreType.DMA((nodes - 1,)),
            pltpu.SemaphoreType.DMA((layers - 1,)),
            pltpu.SemaphoreType.DMA((layers - 1,)),
            pltpu.SemaphoreType.DMA((layers - 1,)),
            pltpu.SemaphoreType.DMA((layers - 1,)),
            pltpu.SemaphoreType.DMA((nodes - 1,)),
            pltpu.SemaphoreType.DMA((nodes - 1,)),
        ],
        compiler_params=pltpu.CompilerParams(
            collective_id=0, has_side_effects=True, vmem_limit_bytes=55 * 1024 * 1024
        ),
        name="gram_sums",
    )(
        snapshots,
        kappa,
    )
    if summed:
        return result.T
    mine = lax.psum_scatter(result, "node", scatter_dimension=0, tiled=True)
    return lax.psum_scatter(mine, "space", scatter_dimension=1, tiled=True) * scale


def solution(mesh):
    placed = (P("node", "space", None), P("space", None))
    return jax.shard_map(
        per_device, mesh=mesh, in_specs=placed, out_specs=P("node", "space"), check_vma=False
    )
```
